256 devices in a mesh: ep: 64 (over x_lo, y, z), dp: 4 (over x_hi, core).
Axes of the slice: x: 4 (x_hi: 2, x_lo: 2; x = x_hi * 2 + x_lo), y: 4, z: 8, core: 2. Of those that a mesh axis runs over, the one named last changes fastest.
Arguments:
- tokens: bfloat16 [32768, 3584], P(('ep', 'dp')), may hold values from -6 to 6
- cotangent: bfloat16 [32768, 3584], P(('ep', 'dp')), may hold values from -6 to 6
- routes: int32 [32768, 1], P(('ep', 'dp')), may hold values from 0 to 63; in each aligned block of 128 rows (0 to 127, 128 to 255, ...) at most 3 rows name the same one
- router_probs: float32 [32768, 1], P(('ep', 'dp')), may hold values from 0.1 to 1
- up_weight: bfloat16 [64, 3584, 1024], P('ep', None, 'dp'), may hold values from -0.09375 to 0.09375
- down_weight: bfloat16 [64, 1024, 3584], P('ep', 'dp'), may hold values from -0.1875 to 0.1875
- moving: int32 [32], replicated, may hold values 0 or 1
Outputs:
- outputs: bfloat16 [32768, 3584], P(('ep', 'dp'))
- input_grad: bfloat16 [32768, 3584], P(('ep', 'dp'))
- up_grad: bfloat16 [64, 3584, 1024], P('ep', None, 'dp')
- down_grad: bfloat16 [64, 1024, 3584], P('ep', 'dp')
The draws below stay inside these ranges and needn't reach their ends.
Inputs may be any that keep to these rules, and one draw needn't show every extreme that they name: `routes`: within each device's aligned block of 128 rows, no expert is named by more than 3 rows, a bound that some block reaches.
All inputs are finite; a program needn't handle non-finite values.
Results may differ from the reference program's by a relative error of at most 0.0095.
Values may be sent and summed in bfloat16 or wider, within the bound.
A program may use at most 128 MiB of HBM per device.

```python
import math
import jax
import jax.numpy as jnp
import numpy as np
from jax import lax

D = 3584
HID = 1024
TOPK = 1
TOK_DEV = 128
EXPERTS = 64
CAP = 3
TOKENS = 32768
N_EP = 64
N_DP = 4


def place_ends(entries, stream_key, low, high):
    shape = entries.shape
    place = [jax.random.randint(jax.random.fold_in(stream_key, axis), (), 0, shape[axis]) for axis in range(len(shape))]
    entries = entries.at[tuple(place)].set(low)
    longest = shape.index(max(shape))
    place[longest] = (place[longest] + 1) % shape[longest]
    return entries.at[tuple(place)].set(high)


def block_levels(stream_key, extent, pieces, least, top_value):
    level, own = 1.0, jax.random.fold_in(stream_key, 6)
    for axis_at, shards_of in pieces:
        draws = jnp.exp(jax.random.uniform(jax.random.fold_in(own, axis_at), (shards_of,), jnp.float32, least / len(pieces), top_value / len(pieces)))
        level = level * jnp.repeat(draws, extent[axis_at] // shards_of).reshape([-1 if axis == axis_at else 1 for axis in range(len(extent))])
    return level


def assign_block(stream_key, own, number, rows, amount, top, most, lean):
    ranking = jax.random.permutation(stream_key, amount)
    heavy_load, usual = load_shares(amount, rows * top, most, lean, True), load_shares(amount, rows * top, most, lean, False)
    places = jnp.arange(amount)

    def named(tallies, rotation):
        used = int((tallies > 0).sum())
        fixed = max(1, used // 4)
        moved = fixed + (places - fixed + rotation * (used - fixed)) % max(1, amount - fixed)
        return jnp.zeros((amount,), jnp.int32).at[ranking[jnp.where(places < fixed, places, moved)]].set(jnp.asarray(tallies, jnp.int32))

    tallies = jnp.where(number % 4 == 0, named(heavy_load, number // 4), named(usual, number - number // 4 - 1))
    mixed = jax.random.permutation(jax.random.fold_in(own, 3), amount)
    giver, receiver = mixed[0:amount // 2 * 2:2], mixed[1:amount // 2 * 2:2]
    slack = jnp.minimum(tallies[giver] - 1, most - tallies[receiver]) // 2
    slack = jnp.where((giver == ranking[0]) | (receiver == ranking[0]) | (tallies[receiver] == 0), 0, jnp.maximum(slack, 0))
    moved = jax.random.randint(jax.random.fold_in(own, 4), (amount // 2,), 0, 1 << 20) % (slack + 1)
    tallies = tallies.at[giver].add(-moved).at[receiver].add(moved)
    labels = jnp.searchsorted(jnp.cumsum(tallies), jnp.arange(rows * top), side="right").astype(jnp.int32)
    listing = labels.reshape(top, rows).T
    listing = listing[jax.random.permutation(jax.random.fold_in(own, 1), rows)]
    rotation = jax.random.randint(jax.random.fold_in(own, 2), (rows, 1), 0, top)
    return jnp.take_along_axis(listing, (jnp.arange(top)[None, :] + rotation) % top, axis=1)


def load_shares(count, total, most, lean, full):
    portions = [(1 << 20) // math.isqrt(standing ** lean) + 1 for standing in range(1, count + 1)]
    largest = most if full else min(most, max(-(-total // count), total * portions[0] // sum(portions)))
    least = 1 if total - largest >= count - 1 else 0
    counts, surplus = [largest] + [least] * (count - 1), total - largest - least * (count - 1)
    while surplus > 0:
        free = [i for i in range(1, count) if counts[i] < largest] or [i for i in range(1, count) if counts[i] < most]
        whole, budget = sum([portions[i] for i in free]), surplus
        for i in free:
            extra = min(most - counts[i], max(1, budget * portions[i] // whole), surplus)
            counts[i] = counts[i] + extra
            surplus = surplus - extra
    return np.array(counts)


def centred(rng, dims, width, reach, cuts=(), held_as=jnp.bfloat16):
    gain = block_levels(rng, dims, cuts, -0.22, 0.18) if cuts else 1.0
    drawn = jax.random.normal(rng, dims, jnp.float32) * width * gain
    return jnp.minimum(jnp.maximum(drawn, -reach), reach).astype(held_as)


def setup_inputs(seed: int = 0) -> dict:
    keys = jax.random.split(jax.random.key(seed), 8)
    tokens = centred(keys[0], (TOKENS, D), 1.0, 6.0, ((0, 256),))
    cotangent = centred(keys[1], (TOKENS, D), 1.0, 6.0, ((0, 256),))
    routes_keys = jax.random.split(jax.random.fold_in(keys[2], 1), TOKENS // TOK_DEV)
    routes_turns = jax.random.permutation(jax.random.fold_in(keys[2], 3), TOKENS // TOK_DEV)
    routes = jax.vmap(lambda own, number: assign_block(jax.random.fold_in(keys[2], 2), own, number, TOK_DEV, EXPERTS, TOPK, CAP, 2))(routes_keys, routes_turns).reshape((TOKENS, TOPK))
    router_probs = jnp.clip(jnp.exp(math.log(1.0) - 2.3025851 * jax.random.uniform(keys[3], (TOKENS, TOPK), jnp.float32) ** block_levels(keys[3], (TOKENS, TOPK), ((0, 256),), -0.2, 0.2)), 0.1, 1.0)
    up_weight = centred(keys[4], (EXPERTS, D, HID), D ** -0.5, 0.09375, ((0, 64), (2, 4)))
    down_weight = centred(keys[5], (EXPERTS, HID, D), HID ** -0.5, 0.1875, ((0, 64), (1, 4)))
    moving = place_ends((jax.random.randint(keys[6], (EXPERTS // 2,), 0, 2) < 1).astype(jnp.int32), jax.random.fold_in(keys[6], 1), 0, 1)
    return dict(tokens=tokens, cotangent=cotangent, routes=routes, router_probs=router_probs, up_weight=up_weight, down_weight=down_weight, moving=moving)


def silu_grad(preact):
    sigmoid = jax.nn.sigmoid(preact)
    return sigmoid * (1.0 + preact * (1.0 - sigmoid))

def rounded_sum(parts):
    rounded = lax.optimization_barrier(parts.astype(jnp.bfloat16))
    return lax.optimization_barrier(jnp.sum(rounded.astype(jnp.float32), axis=0))

def reference(tokens, cotangent, routes, router_probs, up_weight, down_weight, moving):
    half_count = EXPERTS // 2
    buffer_rows = N_DP * N_EP * CAP
    hidden_share = HID // N_DP
    expert_of = routes[:, 0].astype(jnp.int32)
    router_weight = router_probs[:, 0]
    scaled_grad = (router_weight[:, None] * cotangent.astype(jnp.float32)).astype(jnp.bfloat16)
    one_hot = (expert_of[:, None] == jnp.arange(EXPERTS, dtype=jnp.int32)[None, :]).astype(jnp.int32)
    slot_rank = lax.optimization_barrier(jnp.sum(one_hot * (jnp.cumsum(one_hot, axis=0) - 1), axis=1)).astype(jnp.int32)
    token_ids = jnp.arange(TOKENS, dtype=jnp.int32)
    table = jnp.zeros((EXPERTS, buffer_rows), jnp.int32).at[expert_of, slot_rank].set(token_ids)
    filled = jnp.zeros((EXPERTS, buffer_rows), jnp.int32).at[expert_of, slot_rank].set(1)

    def one_expert(packed):
        up_matrix, down_matrix, picked, present = packed
        keep = present[:, None] == 1
        routed = jnp.where(keep, tokens[picked], jnp.zeros((), jnp.bfloat16))
        routed_grad = jnp.where(keep, scaled_grad[picked], jnp.zeros((), jnp.bfloat16))
        preact = jnp.dot(routed, up_matrix, preferred_element_type=jnp.float32)
        hidden = jax.nn.silu(preact).astype(jnp.bfloat16)
        hidden_split = hidden.astype(jnp.float32).reshape(buffer_rows, N_DP, hidden_share)
        down_split = down_matrix.astype(jnp.float32).reshape(N_DP, hidden_share, D)
        out_parts = jnp.einsum('rsh,shd->srd', hidden_split, down_split)
        expert_out = rounded_sum(out_parts).astype(jnp.bfloat16)
        hidden_grad = jnp.dot(routed_grad, down_matrix.T, preferred_element_type=jnp.float32)
        preact_grad = (hidden_grad * silu_grad(preact)).astype(jnp.bfloat16)
        grad_split = preact_grad.astype(jnp.float32).reshape(buffer_rows, N_DP, hidden_share)
        up_split = up_matrix.astype(jnp.float32).reshape(D, N_DP, hidden_share)
        input_parts = jnp.einsum('rsh,dsh->srd', grad_split, up_split)
        routed_input = rounded_sum(input_parts).astype(jnp.bfloat16)
        grad_up = jnp.dot(routed.T, preact_grad, preferred_element_type=jnp.float32).astype(jnp.bfloat16)
        grad_down = jnp.dot(hidden.T, routed_grad, preferred_element_type=jnp.float32).astype(jnp.bfloat16)
        return (expert_out, routed_input, grad_up, grad_down)
    expert_out, routed_input, grad_up, grad_down = lax.map(one_expert, (up_weight, down_weight, table, filled))
    mixed = expert_out[expert_of, slot_rank]
    outputs = (router_weight[:, None] * mixed.astype(jnp.float32)).astype(jnp.bfloat16)
    input_grad = routed_input[expert_of, slot_rank]
    device_ids = jnp.arange(EXPERTS, dtype=jnp.int32)
    pair_flag = moving[device_ids % half_count]
    partner = jnp.where(device_ids < half_count, device_ids + half_count, device_ids - half_count)
    held = jnp.where(pair_flag == 1, partner, device_ids).astype(jnp.int32)
    return (outputs, input_grad, grad_up[held], grad_down[held])
```

```python
import jax
import jax.numpy as jnp
from jax import lax
from jax.sharding import PartitionSpec as P


def swapped_2(value, axis, bit):
    return lax.ppermute(value, axis, [(i, i ^ 1 << bit) for i in range(lax.axis_size(axis))])


def silu_grad(preact):
    sigmoid = jax.nn.sigmoid(preact)
    return sigmoid * (1.0 + preact * (1.0 - sigmoid))


def contract_rows(left, right):
    return lax.dot_general(
        left, right, (((0,), (0,)), ((), ())), preferred_element_type=jnp.float32
    )


def contract_cols(left, right):
    return lax.dot_general(
        left, right, (((1,), (1,)), ((), ())), preferred_element_type=jnp.float32
    )


def shards(tokens, cotangent, routes, router_probs, up_weight, down_weight, moving):
    ep_count = lax.axis_size("ep")
    dp_count = lax.axis_size("dp")
    half_count = ep_count // 2
    high_bit = ep_count.bit_length() - 2
    token_count = tokens.shape[0]
    feature_count = tokens.shape[1]
    capacity = 3 * token_count * routes.shape[1] // (2 * ep_count)
    slot_count = ep_count * capacity
    ep_index = lax.axis_index("ep")
    pair_ids = jnp.arange(half_count, dtype=jnp.int32)
    swapped = jnp.sum(jnp.where(pair_ids == ep_index % half_count, moving, 0)) == 1
    expert_of = routes[:, 0]
    router_weight = router_probs[:, 0]
    expert_flip = (
        jnp.sum(
            jnp.where((expert_of % half_count)[:, None] == pair_ids[None, :], moving[None, :], 0),
            axis=1,
        )
        == 1
    )
    partner = jnp.where(expert_of < half_count, expert_of + half_count, expert_of - half_count)
    target = jnp.where(expert_flip, partner, expert_of)
    other_up, other_down = swapped_2((up_weight, down_weight), "ep", high_bit)
    up_matrix = jnp.where(swapped, other_up, up_weight)[0]
    down_matrix = jnp.where(swapped, other_down, down_weight)[0]
    order = jnp.arange(token_count, dtype=jnp.int32)
    slot_rank = jnp.sum(
        ((target[:, None] == target[None, :]) & (order[None, :] < order[:, None])).astype(jnp.int32),
        axis=1,
    )
    slot_of = target * capacity + slot_rank
    select = (jnp.arange(slot_count, dtype=jnp.int32)[:, None] == slot_of[None, :]).astype(
        jnp.bfloat16
    )
    scaled_grad = (router_weight[:, None] * cotangent.astype(jnp.float32)).astype(jnp.bfloat16)
    token_buffer = jnp.dot(select, tokens, preferred_element_type=jnp.float32).astype(jnp.bfloat16)
    grad_buffer = jnp.dot(select, scaled_grad, preferred_element_type=jnp.float32).astype(
        jnp.bfloat16
    )
    token_buffer = token_buffer.reshape(ep_count, capacity, feature_count)
    grad_buffer = grad_buffer.reshape(ep_count, capacity, feature_count)
    arrived, arrived_grad = (
        lax.all_to_all(token_buffer, "ep", split_axis=0, concat_axis=0, tiled=True),
        lax.all_to_all(grad_buffer, "ep", split_axis=0, concat_axis=0, tiled=True),
    )
    routed, routed_grad = (
        lax.all_gather(arrived, "dp", axis=0, tiled=True),
        lax.all_gather(arrived_grad, "dp", axis=0, tiled=True),
    )
    row_count = dp_count * slot_count
    routed = routed.reshape(row_count, feature_count)
    routed_grad = routed_grad.reshape(row_count, feature_count)
    preact = jnp.dot(routed, up_matrix, preferred_element_type=jnp.float32)
    hidden = jax.nn.silu(preact).astype(jnp.bfloat16)
    out_part = jnp.dot(hidden, down_matrix, preferred_element_type=jnp.float32)
    out_part = out_part.reshape(dp_count * ep_count, capacity, feature_count)
    hidden_grad = contract_cols(routed_grad, down_matrix)
    preact_grad = (hidden_grad * silu_grad(preact)).astype(jnp.bfloat16)
    input_part = contract_cols(preact_grad, up_matrix)
    input_part = input_part.reshape(dp_count * ep_count, capacity, feature_count)
    out_sum, input_sum = (
        lax.psum_scatter(
            out_part.astype(jnp.bfloat16), "dp", scatter_dimension=0, tiled=True
        ).astype(jnp.float32),
        lax.psum_scatter(
            input_part.astype(jnp.bfloat16), "dp", scatter_dimension=0, tiled=True
        ).astype(jnp.float32),
    )
    out_back, input_back = (
        lax.all_to_all(out_sum.astype(jnp.bfloat16), "ep", split_axis=0, concat_axis=0, tiled=True),
        lax.all_to_all(
            input_sum.astype(jnp.bfloat16), "ep", split_axis=0, concat_axis=0, tiled=True
        ),
    )
    up_grad = contract_rows(routed, preact_grad).astype(jnp.bfloat16)[None]
    down_grad = contract_rows(hidden, routed_grad).astype(jnp.bfloat16)[None]
    mixed = contract_rows(select, out_back.reshape(slot_count, feature_count))
    outputs = (router_weight[:, None] * mixed).astype(jnp.bfloat16)
    input_grad = contract_rows(select, input_back.reshape(slot_count, feature_count)).astype(
        jnp.bfloat16
    )
    return (outputs, input_grad, up_grad, down_grad)


def solution(mesh):
    in_specs = (
        P(("ep", "dp"), None),
        P(("ep", "dp"), None),
        P(("ep", "dp"), None),
        P(("ep", "dp"), None),
        P("ep", None, "dp"),
        P("ep", "dp", None),
        P(),
    )
    out_specs = (
        P(("ep", "dp"), None),
        P(("ep", "dp"), None),
        P("ep", None, "dp"),
        P("ep", "dp", None),
    )
    return jax.shard_map(shards, mesh=mesh, in_specs=in_specs, out_specs=out_specs, check_vma=False)
```

```python
import functools

import jax
import jax.numpy as jnp
import numpy as np
from jax import lax
from jax.experimental import pallas as pl
from jax.experimental.pallas import tpu as pltpu
from jax.sharding import PartitionSpec as P

MESH = pl.DeviceIdType.MESH
NX = 4
CAP = 3
BF16 = jnp.bfloat16
F32 = jnp.float32


def dot(left, right, dims=((1,), (0,))):
    return lax.dot_general(left, right, (dims, ((), ())), preferred_element_type=F32)


def columns(width, parts, body):
    step = width // parts

    def run(i, _):
        body(pl.ds(pl.multiple_of(i * step, step), step))
        return 0

    lax.fori_loop(0, parts, run, 0)


class Geometry:
    def __init__(self, ny, nz):
        self.ny, self.nz = ny, nz
        self.zrows = 2 * ny * 2 * CAP
        self.yrows = 2 * nz * CAP
        self.xrows = ny * nz * CAP
        self.rows = 2 * self.xrows

    def matrices(self):
        ny, nz, rows = self.ny, self.nz, self.rows
        by_z = np.arange(rows).reshape(nz, ny, 2, CAP)
        by_y = by_z.transpose(1, 2, 0, 3).reshape(-1)
        per_z = ny * 2 * CAP
        split = lambda source, h: (source // per_z) * 2 * per_z + h * per_z + source % per_z
        to_y = np.zeros((2, rows, 2 * rows), np.float32)
        for h in range(2):
            to_y[h, np.arange(rows), split(by_y, h)] = 1
        at_y = np.arange(rows).reshape(ny, 2, nz, CAP)
        by_r = at_y.transpose(1, 0, 2, 3).reshape(-1)
        to_x = np.zeros((rows, rows), np.float32)
        to_x[np.arange(rows), by_r] = 1
        return [
            m.astype(jnp.bfloat16)
            for m in (to_y, to_y.transpose(0, 2, 1), to_x, to_x.T)
        ]


def kernel(
    geo,
    tokens,
    cotangent,
    weight,
    select,
    unselect,
    to_y,
    from_y,
    to_x,
    from_x,
    flag,
    up_own,
    down_own,
    outputs,
    input_grad,
    up_grad,
    down_grad,
    up,
    down,
    preact,
    hidden,
    slope,
    sent,
    got_z,
    got_y,
    routed,
    part,
    core_part,
    x_part,
    back_y,
    back_z,
    send_sem,
    recv_sem,
    out_sem,
):
    ny, nz = geo.ny, geo.nz
    xr, yr, zr, rows = geo.xrows, geo.yrows, geo.zrows, geo.rows
    width = tokens.shape[1]
    half = width // 2
    ep, dp = lax.axis_index("ep"), lax.axis_index("dp")
    x_lo, y, z = ep // (ny * nz), (ep // nz) % ny, ep % nz
    x, core = (dp // 2) * 2 + x_lo, dp % 2

    def at(dx=0, dy=0, dz=0, dc=0):
        nx_, ny_, nz_ = (x + dx) % NX, (y + dy % ny) % ny, (z + dz % nz) % nz
        return ((nx_ % 2) * (ny * nz) + ny_ * nz + nz_, (nx_ // 2) * 2 + (core + dc) % 2)

    used = {}

    def remote(key, src, dst, device):
        number = used.setdefault(key, len(used))
        return pltpu.make_async_remote_copy(
            src_ref=src,
            dst_ref=dst,
            send_sem=send_sem.at[number],
            recv_sem=recv_sem.at[number],
            device_id=device,
            device_id_type=MESH,
        )

    peers = (
        [at(dz=d) for d in range(1, nz)]
        + [at(dy=d) for d in range(1, ny)]
        + [at(dx=d) for d in range(1, NX)]
        + [at(dc=1)]
    )
    barrier = pltpu.get_barrier_semaphore()
    for peer in peers:
        pl.semaphore_signal(barrier, inc=1, device_id=peer, device_id_type=MESH)
    pl.semaphore_wait(barrier, len(peers))

    waiting = {}

    def start(copy):
        copy.start()
        waiting[id(copy)] = copy
        return copy

    def settle(copies):
        for copy in copies:
            copy.wait_send()
            del waiting[id(copy)]

    def z_block(d):
        return pl.ds(d * zr, zr)

    def y_block(d):
        return pl.ds(d * yr, yr)

    def x_block(d):
        return pl.ds(d * xr, xr)

    def pick(s):
        def tile(cols):
            far = pl.ds(cols.start + half, cols.size)
            if s == 0:
                near_part, far_part = tokens[:, cols], tokens[:, far]
            else:
                near_part = (weight[...] * cotangent[:, cols].astype(F32)).astype(BF16)
                far_part = (weight[...] * cotangent[:, far].astype(F32)).astype(BF16)
            both = jnp.concatenate([near_part, far_part], axis=0)
            sent[s, :, cols] = dot(select[...], both).astype(BF16)

        columns(half, 7, tile)
        got_z[s, z_block(0), :] = sent[s, z_block(0), :]
        return [
            start(remote(("z", s, d), sent.at[s, z_block(d)], got_z.at[s, z_block(d)], at(dz=d)))
            for d in range(1, nz)
        ]

    def to_ring_y(s, copies):
        for copy in copies:
            copy.wait_recv()

        def tile(cols):
            block = got_z[s, :, cols]
            far = pl.ds(cols.start + half, cols.size)
            part[s, pl.ds(0, rows), cols] = dot(to_y[0], block).astype(BF16)
            part[s, pl.ds(0, rows), far] = dot(to_y[1], block).astype(BF16)

        columns(half, 7, tile)
        got_y[s, y_block(0), :] = part[s, y_block(0), :]
        return [
            start(remote(("y", s, d), part.at[s, y_block(d)], got_y.at[s, y_block(d)], at(dy=d)))
            for d in range(1, ny)
        ]

    def to_ring_x(s, copies):
        for copy in copies:
            copy.wait_recv()

        def tile(cols):
            block = dot(to_x[...], got_y[s, :, cols]).astype(BF16)
            routed[s, x_block(0), cols] = block[:xr]
            part[s, pl.ds(rows, xr), cols] = block[xr:]

        columns(width, 7, tile)
        other = part.at[s, pl.ds(rows, xr)]
        own = routed.at[s, x_block(0)]
        made = {
            1: start(remote(("x", s, 1), other, routed.at[s, x_block(2)], at(dx=1))),
            3: start(remote(("x", s, 3), other, routed.at[s, x_block(6)], at(dx=3))),
            2: start(remote(("x", s, 2), own, routed.at[s, x_block(4)], at(dx=2))),
            0: start(remote(("c", s, 0), own, routed.at[s, x_block(1)], at(dc=1))),
        }
        return made

    def share(s, made):
        shared = {0: made[0]}
        for d in (1, 3, 2):
            made[d].wait_recv()
            block = routed.at[s, x_block(2 * d)]
            shared[d] = start(
                remote(("c", s, d), block, routed.at[s, x_block(2 * d + 1)], at(dc=1))
            )
        return shared

    def take_weights(swaps):
        chosen = flag[0] == 1
        for copy, buffer, own, parts in zip(swaps, (up, down), (up_own, down_own), (7, 4)):
            copy.wait_recv()
            step = buffer.shape[0] // parts

            def run(i, _, buffer=buffer, own=own, step=step):
                at_rows = pl.ds(pl.multiple_of(i * step, step), step)
                buffer[at_rows, :] = lax.select(chosen, buffer[at_rows, :], own[at_rows, :])
                return 0

            lax.fori_loop(0, parts, run, 0)

    def send_core(s, d):
        return start(
            remote(
                ("p", s, d), part.at[s, x_block(2 * d + 1)], core_part.at[s, x_block(d)], at(dc=1)
            )
        )

    def forward(shared):
        made = {}
        for d in (0, 1, 3, 2):
            shared[d].wait_recv()
            pair = pl.ds(2 * d * xr, 2 * xr)
            value = dot(routed[0, pair, :], up[...])
            sigmoid = jax.nn.sigmoid(value)
            active = (value * sigmoid).astype(BF16)
            slope[pair, :] = sigmoid * (1.0 + value * (1.0 - sigmoid))
            hidden[pair, :] = active

            def tile(cols, active=active, pair=pair):
                part[0, pair, cols] = dot(active, down[:, cols]).astype(BF16)

            columns(width, 7, tile)
            made[d] = send_core(0, d)
        return made

    def backward(shared):
        made = {}
        for d in (0, 1, 3, 2):
            shared[d].wait_recv()
            pair = pl.ds(2 * d * xr, 2 * xr)
            value = dot(routed[1, pair, :], down[...], ((1,), (1,)))
            grad = (value * slope[pair, :]).astype(BF16)
            preact[pair, :] = grad

            def tile(i, _, grad=grad, pair=pair):
                step = width // 7
                cols = pl.ds(pl.multiple_of(i * step, step), step)
                part[1, pair, cols] = dot(grad, up[cols, :], ((1,), (1,))).astype(BF16)
                return 0

            lax.fori_loop(0, 7, tile, 0)
            made[d] = send_core(1, d)
        return made

    def add_into(target, s, first, other, second):
        def tile(cols):
            total = target[s, first, cols].astype(F32) + other[s, second, cols].astype(F32)
            target[s, first, cols] = total.astype(BF16)

        columns(width, 7, tile)

    def chip_sums(s, made):
        back = {}
        for d, place in ((1, 1), (3, 2), (2, 0), (0, None)):
            made[d].wait_recv()
            add_into(part, s, x_block(2 * d), core_part, x_block(d))
            if d:
                back[d] = start(
                    remote(
                        ("b", s, d),
                        part.at[s, x_block(2 * d)],
                        x_part.at[s, x_block(place)],
                        at(dx=NX - d),
                    )
                )
        return back

    def from_ring_x(s, back):
        for d in (1, 3, 2):
            back[d].wait_recv()

        def tile(cols):
            same = part[s, x_block(0), cols].astype(F32) + x_part[s, x_block(0), cols].astype(F32)
            cross = x_part[s, x_block(1), cols].astype(F32) + x_part[s, x_block(2), cols].astype(F32)
            both = jnp.concatenate([same.astype(BF16), cross.astype(BF16)], axis=0)
            got_y[s, :, cols] = dot(from_x[...], both).astype(BF16)

        columns(width, 7, tile)
        back_y[s, y_block(0), :] = got_y[s, y_block(0), :]
        return [
            start(remote(("v", s, d), got_y.at[s, y_block(d)], back_y.at[s, y_block(d)], at(dy=-d)))
            for d in range(1, ny)
        ]

    def from_ring_y(s, copies, dispatched):
        for copy in copies:
            copy.wait_recv()
        settle(dispatched)

        def tile(cols):
            far = pl.ds(cols.start + half, cols.size)
            near_rows = dot(from_y[0], back_y[s, :, cols])
            far_rows = dot(from_y[1], back_y[s, :, far])
            sent[s, :, cols] = (near_rows + far_rows).astype(BF16)

        columns(half, 7, tile)
        back_z[s, z_block(0), :] = sent[s, z_block(0), :]
        return [
            start(remote(("w", s, d), sent.at[s, z_block(d)], back_z.at[s, z_block(d)], at(dz=-d)))
            for d in range(1, nz)
        ]

    def finish(s, copies, out):
        for copy in copies:
            copy.wait_recv()
        count = tokens.shape[0]

        def tile(cols):
            for h in range(2):
                place = pl.ds(cols.start + h * half, cols.size)
                picked = dot(unselect[pl.ds(h * count, count), :], back_z[s, :, cols])
                out[:, place] = (picked if s else weight[...] * picked).astype(BF16)

        columns(half, 7, tile)

    z_t = pick(0)
    swaps = [
        start(remote(("s", i), own, buffer, at(dx=1 + 2 * x_lo)))
        for i, (own, buffer) in enumerate(((up_own, up), (down_own, down)))
    ]
    z_g = pick(1)
    y_t = to_ring_y(0, z_t)
    x_t = to_ring_x(0, y_t)
    y_g = to_ring_y(1, z_g)
    shared_t = share(0, x_t)
    x_g = to_ring_x(1, y_g)
    take_weights(swaps)
    settle(y_t + [x_t[1], x_t[3]])
    made_t = forward(shared_t)
    shared_g = share(1, x_g)
    back_t = chip_sums(0, made_t)
    settle(y_g + [x_g[1], x_g[3]])
    made_g = backward(shared_g)
    v_t = from_ring_x(0, back_t)
    back_g = chip_sums(1, made_g)
    w_t = from_ring_y(0, v_t, z_t)

    def up_tile(i, _):
        step = width // 7
        cols = pl.ds(pl.multiple_of(i * step, step), step)
        up[cols, :] = dot(routed[0, :, cols], preact[...], ((0,), (0,))).astype(BF16)
        return 0

    lax.fori_loop(0, 7, up_tile, 0)
    write_up = pltpu.make_async_copy(up, up_grad, out_sem.at[0])
    write_up.start()
    v_g = from_ring_x(1, back_g)
    w_g = from_ring_y(1, v_g, z_g)

    def down_tile(cols):
        down[:, cols] = dot(hidden[...], routed[1, :, cols], ((0,), (0,))).astype(BF16)

    columns(width, 7, down_tile)
    write_down = pltpu.make_async_copy(down, down_grad, out_sem.at[1])
    write_down.start()
    finish(0, w_t, outputs)
    finish(1, w_g, input_grad)
    settle(list(waiting.values()))
    write_up.wait()
    write_down.wait()


def shards(geo, tokens, cotangent, routes, router_probs, up_weight, down_weight, moving):
    ny, nz = geo.ny, geo.nz
    count, width = tokens.shape
    hid = up_weight.shape[2]
    half_count = ny * nz
    rows, xr = geo.rows, geo.xrows
    ep_index = lax.axis_index("ep")
    pair_ids = jnp.arange(half_count, dtype=jnp.int32)
    swapped = jnp.sum(jnp.where(pair_ids == ep_index % half_count, moving, 0), keepdims=True)
    expert_of = routes[:, 0]
    flip = jnp.sum(
        jnp.where((expert_of % half_count)[:, None] == pair_ids[None, :], moving[None, :], 0), axis=1
    )
    target = (expert_of + half_count * flip) % (2 * half_count)
    order = jnp.arange(count, dtype=jnp.int32)
    rank = jnp.sum(
        ((target[:, None] == target[None, :]) & (order[None, :] < order[:, None])).astype(jnp.int32),
        axis=1,
    )
    dz = (target % nz - ep_index % nz + nz) % nz
    dy = (target // nz % ny - ep_index // nz % ny + ny) % ny
    cross = (target // half_count + ep_index // half_count) % 2
    near = dz * geo.zrows + (dy * 2 + cross) * CAP + rank
    slot = jnp.concatenate([near, near + geo.zrows // 2])
    place = jnp.arange(2 * rows, dtype=jnp.int32)
    select = (place[:, None] == slot[None, :]).astype(BF16)
    unselect = (slot[:, None] == place[None, :]).astype(BF16)
    vmem = pl.BlockSpec(memory_space=pltpu.VMEM)
    copies = 2 * (2 * (nz - 1) + 2 * (ny - 1) + 3 + 4 + 4 + 3) + 2
    buffer = lambda *shape: pltpu.VMEM(shape, BF16)
    outputs, input_grad, up_grad, down_grad = pl.pallas_call(
        functools.partial(kernel, geo),
        out_shape=(
            jax.ShapeDtypeStruct((count, width), BF16),
            jax.ShapeDtypeStruct((count, width), BF16),
            jax.ShapeDtypeStruct((width, hid), BF16),
            jax.ShapeDtypeStruct((hid, width), BF16),
        ),
        in_specs=[vmem] * 9 + [pl.BlockSpec(memory_space=pltpu.SMEM)] + [vmem] * 2,
        out_specs=(vmem, vmem) + (pl.BlockSpec(memory_space=pl.ANY),) * 2,
        scratch_shapes=[
            buffer(width, hid),
            buffer(hid, width),
            buffer(8 * xr, hid),
            buffer(8 * xr, hid),
            pltpu.VMEM((8 * xr, hid), F32),
            buffer(2, 2 * rows, width // 2),
            buffer(2, 2 * rows, width // 2),
            buffer(2, rows, width),
            buffer(2, 8 * xr, width),
            buffer(2, 8 * xr, width),
            buffer(2, 4 * xr, width),
            buffer(2, 3 * xr, width),
            buffer(2, rows, width),
            buffer(2, 2 * rows, width // 2),
            pltpu.SemaphoreType.DMA((copies,)),
            pltpu.SemaphoreType.DMA((copies,)),
            pltpu.SemaphoreType.DMA((2,)),
        ],
        compiler_params=pltpu.CompilerParams(
            collective_id=0, has_side_effects=True, vmem_limit_bytes=63 * 2**20
        ),
    )(
        tokens,
        cotangent,
        router_probs,
        select,
        unselect,
        *[jnp.asarray(m) for m in geo.matrices()],
        swapped,
        up_weight[0],
        down_weight[0],
    )
    return outputs, input_grad, up_grad[None], down_grad[None]


def solution(mesh):
    ep_count = mesh.shape["ep"]
    nz = 8 if ep_count == 64 else 2
    geo = Geometry(ep_count // 2 // nz, nz)
    in_specs = (
        P(("ep", "dp"), None),
        P(("ep", "dp"), None),
        P(("ep", "dp"), None),
        P(("ep", "dp"), None),
        P("ep", None, "dp"),
        P("ep", "dp", None),
        P(),
    )
    out_specs = (
        P(("ep", "dp"), None),
        P(("ep", "dp"), None),
        P("ep", None, "dp"),
        P("ep", "dp", None),
    )
    return jax.shard_map(
        functools.partial(shards, geo),
        mesh=mesh,
        in_specs=in_specs,
        out_specs=out_specs,
        check_vma=False,
    )
```

```python
import functools

import jax
import jax.numpy as jnp
import numpy as np
from jax import lax
from jax.experimental import pallas as pl
from jax.experimental.pallas import tpu as pltpu
from jax.sharding import PartitionSpec as P

MESH = pl.DeviceIdType.MESH
NX = 4
CAP = 3
CHUNKS = 4
BF16 = jnp.bfloat16
F32 = jnp.float32
I32 = jnp.int32


def dot(left, right, dims=((1,), (0,))):
    return lax.dot_general(left, right, (dims, ((), ())), preferred_element_type=F32)


def loop(count, body):
    def run(i, _):
        body(i)
        return 0

    lax.fori_loop(0, count, run, 0)


class Geometry:
    def __init__(self, ny, nz):
        self.ny, self.nz = ny, nz
        self.zrows = ny * 2 * CAP
        self.yrows = 2 * nz * CAP
        self.xrows = ny * nz * CAP
        self.rows = 2 * self.xrows

    def matrices(self):
        ny, nz, rows = self.ny, self.nz, self.rows
        by_z = np.arange(rows).reshape(nz, ny, 2, CAP)
        by_y = np.arange(rows).reshape(ny, 2, nz, CAP)
        to_y = np.zeros((rows, rows), np.float32)
        to_y[np.arange(rows), by_z.transpose(1, 2, 0, 3).reshape(-1)] = 1
        to_x = np.zeros((rows, rows), np.float32)
        to_x[np.arange(rows), by_y.transpose(1, 0, 2, 3).reshape(-1)] = 1
        return [m.astype(jnp.bfloat16) for m in (to_y, to_y.T, to_x, to_x.T)]


def kernel(
    geo,
    tokens_in,
    cotangent_in,
    routes,
    probs,
    moving,
    up_in,
    down_in,
    to_y,
    from_y,
    to_x,
    from_x,
    outputs,
    input_grad,
    up_grad,
    down_grad,
    tokens,
    cotangent,
    up_own,
    down_own,
    up,
    down,
    hidden_grad,
    hidden,
    slope,
    select,
    unselect,
    sent,
    got_z,
    got_y,
    routed,
    part,
    core_part,
    x_part,
    back_y,
    back_z,
    send_sem,
    recv_sem,
    local_sem,
):
    ny, nz = geo.ny, geo.nz
    xr, yr, zr, rows = geo.xrows, geo.yrows, geo.zrows, geo.rows
    count, width = tokens.shape
    wide = width // CHUNKS
    ep, dp = lax.axis_index("ep"), lax.axis_index("dp")
    x_lo, y, z = ep // (ny * nz), (ep // nz) % ny, ep % nz
    x, core = (dp // 2) * 2 + x_lo, dp % 2

    def at(dx=0, dy=0, dz=0, dc=0):
        nx_, ny_, nz_ = (x + dx) % NX, (y + dy % ny) % ny, (z + dz % nz) % nz
        return ((nx_ % 2) * (ny * nz) + ny_ * nz + nz_, (nx_ // 2) * 2 + (core + dc) % 2)

    peers = (
        [at(dz=d) for d in range(1, nz)]
        + [at(dy=d) for d in range(1, ny)]
        + [at(dx=d) for d in range(1, NX)]
        + [at(dc=1)]
    )
    barrier = pltpu.get_barrier_semaphore()
    for peer in peers:
        pl.semaphore_signal(barrier, inc=1, device_id=peer, device_id_type=MESH)

    loads = [
        pltpu.make_async_copy(src, dst, local_sem.at[i])
        for i, (src, dst) in enumerate(
            (
                (tokens_in, tokens),
                (cotangent_in, cotangent),
                (up_in, up_own),
                (down_in, down_own),
            )
        )
    ]
    for load in loads:
        load.start()

    used = {}
    waiting = {}

    def start(key, src, dst, device):
        number = used.setdefault(key, len(used))
        copy = pltpu.make_async_remote_copy(
            src_ref=src,
            dst_ref=dst,
            send_sem=send_sem.at[number],
            recv_sem=recv_sem.at[number],
            device_id=device,
            device_id_type=MESH,
        )
        copy.start()
        waiting[id(copy)] = copy
        return copy

    def settle(copies):
        for copy in copies:
            copy.wait_send()
            del waiting[id(copy)]

    def y_block(d):
        return pl.ds(d * yr, yr)

    def x_block(d):
        return pl.ds(d * xr, xr)

    def chunk_cols(ch):
        return pl.ds(pl.multiple_of(ch * wide, wide), wide)

    half_count = ny * nz
    expert = routes[...]
    flip = jnp.zeros_like(expert)
    for pair in range(half_count):
        flip += jnp.where((expert & (half_count - 1)) == pair, moving[pair], 0)
    target_row = (expert + half_count * flip) & (2 * half_count - 1)
    down_iota = lax.broadcasted_iota(I32, (count, count), 0)
    across_iota = lax.broadcasted_iota(I32, (count, count), 1)

    def as_column(row):
        spread = jnp.where(down_iota == across_iota, row.astype(F32), 0.0)
        return jnp.sum(spread, axis=1, keepdims=True)

    target_column = as_column(target_row).astype(I32)
    same = target_column == target_row
    rank_row = jnp.sum(
        jnp.where(same & (down_iota < across_iota), 1.0, 0.0), axis=0, keepdims=True
    ).astype(I32)

    def slot_of(target, rank):
        dz = (target - z) & (nz - 1)
        dy = (target // nz - y) & (ny - 1)
        cross = (target // half_count) ^ x_lo
        return dz * zr + (dy * 2 + cross) * CAP + rank

    slot_row = slot_of(target_row, rank_row)
    slot_column = as_column(slot_row).astype(I32)
    select[...] = jnp.where(
        lax.broadcasted_iota(I32, (rows, count), 0) == slot_row, 1.0, 0.0
    ).astype(BF16)
    unselect[...] = jnp.where(
        lax.broadcasted_iota(I32, (count, rows), 1) == slot_column, 1.0, 0.0
    ).astype(BF16)
    weight = as_column(probs[...])

    def pick(s):
        loads[s].wait()

        def tile(ch):
            cols = chunk_cols(ch)
            if s == 0:
                given = tokens[:, cols]
            else:
                given = (weight * cotangent[:, cols].astype(F32)).astype(BF16)
            block = dot(select[...], given).astype(BF16)
            for d in range(nz):
                sent[s, ch, d] = block[d * zr : (d + 1) * zr]
            got_z[s, ch, 0] = block[:zr]

        loop(CHUNKS, tile)

    def send_z(s):
        return [
            start(("z", s, d), sent.at[s, :, d], got_z.at[s, :, d], at(dz=d)) for d in range(1, nz)
        ]

    def to_ring_y(s, copies):
        for copy in copies:
            copy.wait_recv()

        def tile(ch):
            block = jnp.concatenate([got_z[s, ch, d] for d in range(nz)], axis=0)
            block = dot(to_y[...], block).astype(BF16)
            part[s, ch, pl.ds(0, rows), :] = block
            got_y[s, ch, y_block(0), :] = block[:yr]

        loop(CHUNKS, tile)
        return [
            start(
                ("y", s, d), part.at[s, :, y_block(d)], got_y.at[s, :, y_block(d)], at(dy=d)
            )
            for d in range(1, ny)
        ]

    def to_ring_x(s, copies):
        for copy in copies:
            copy.wait_recv()

        def tile(ch):
            block = dot(to_x[...], got_y[s, ch]).astype(BF16)
            routed[s, ch, x_block(0), :] = block[:xr]
            part[s, ch, pl.ds(rows, xr), :] = block[xr:]

        loop(CHUNKS, tile)

    def send_x(s):
        other = part.at[s, :, pl.ds(rows, xr)]
        own = routed.at[s, :, x_block(0)]
        return {
            1: start(("x", s, 1), other, routed.at[s, :, x_block(1)], at(dx=1)),
            3: start(("x", s, 3), other, routed.at[s, :, x_block(3)], at(dx=3)),
            2: start(("x", s, 2), own, routed.at[s, :, x_block(2)], at(dx=2)),
            0: start(("c", s, 0), own, routed.at[s, :, x_block(4)], at(dc=1)),
        }

    def share(s, made):
        shared = [made[0]]
        for d in (1, 3, 2):
            made[d].wait_recv()
            shared.append(
                start(
                    ("c", s, d),
                    routed.at[s, :, x_block(d)],
                    routed.at[s, :, x_block(4 + d)],
                    at(dc=1),
                )
            )
        return shared

    def take_weights(swaps):
        chosen = moving[ep % half_count] == 1
        for copy, load, buffer, own, parts in zip(
            swaps, loads[2:], (up, down), (up_own, down_own), (7, 4)
        ):
            load.wait()
            copy.wait_recv()
            step = buffer.shape[0] // parts

            def run(i, buffer=buffer, own=own, step=step):
                at_rows = pl.ds(pl.multiple_of(i * step, step), step)
                buffer[at_rows, :] = lax.select(chosen, buffer[at_rows, :], own[at_rows, :])

            loop(parts, run)

    def group(i):
        return pl.ds(pl.multiple_of(i * 4 * xr, 4 * xr), 4 * xr)

    def forward(shared):
        for copy in shared:
            copy.wait_recv()

        def run(i):
            value = dot(routed[0, 0, group(i), :], up[pl.ds(0, wide), :])
            for ch in range(1, CHUNKS):
                value += dot(routed[0, ch, group(i), :], up[pl.ds(ch * wide, wide), :])
            sigmoid = jax.nn.sigmoid(value)
            hidden[group(i), :] = (value * sigmoid).astype(BF16)
            slope[group(i), :] = sigmoid * (1.0 + value * (1.0 - sigmoid))

        loop(2, run)

    def backward(shared):
        for copy in shared:
            copy.wait_recv()
        over_cols = ((1,), (1,))

        def run(i):
            value = dot(routed[1, 0, group(i), :], down[:, pl.ds(0, wide)], over_cols)
            for ch in range(1, CHUNKS):
                cols = pl.ds(ch * wide, wide)
                value += dot(routed[1, ch, group(i), :], down[:, cols], over_cols)
            hidden_grad[group(i), :] = (value * slope[group(i), :]).astype(BF16)

        loop(2, run)

    def parts(s, ch):
        def run(i):
            if s == 0:
                block = dot(hidden[group(i), :], down[:, pl.ds(ch * wide, wide)])
            else:
                block = dot(
                    hidden_grad[group(i), :], up[pl.ds(ch * wide, wide), :], ((1,), (1,))
                )
            part[s, ch, group(i), :] = block.astype(BF16)

        loop(2, run)
        far = part.at[s, ch, pl.ds(4 * xr, 4 * xr)]
        return start(("p", s, ch), far, core_part.at[s, ch], at(dc=1))

    def chip_sum(s, ch, copy):
        copy.wait_recv()

        def run(i):
            block = x_block_at(i)
            total = part[s, ch, block, :].astype(F32) + core_part[s, ch, block, :].astype(F32)
            part[s, ch, block, :] = total.astype(BF16)

        loop(4, run)
        return [
            start(
                ("b", s, ch, d),
                part.at[s, ch, x_block(d)],
                x_part.at[s, ch, x_block(place)],
                at(dx=NX - d),
            )
            for d, place in ((1, 1), (3, 2), (2, 0))
        ]

    def x_block_at(i):
        return pl.ds(pl.multiple_of(i * xr, xr), xr)

    def from_ring_x(s, ch, copies):
        for copy in copies:
            copy.wait_recv()
        taken = [x_part[s, ch, x_block(i), :].astype(F32) for i in range(3)]
        same_x = (part[s, ch, x_block(0), :].astype(F32) + taken[0]).astype(BF16)
        cross_x = (taken[1] + taken[2]).astype(BF16)
        block = dot(from_x[...], jnp.concatenate([same_x, cross_x], axis=0)).astype(BF16)
        got_y[s, ch] = block
        back_y[s, ch, y_block(0), :] = block[:yr]
        return [
            start(
                ("v", s, ch, d),
                got_y.at[s, ch, y_block(d)],
                back_y.at[s, ch, y_block(d)],
                at(dy=-d),
            )
            for d in range(1, ny)
        ]

    def from_ring_y(s, ch, copies):
        for copy in copies:
            copy.wait_recv()
        block = dot(from_y[...], back_y[s, ch]).astype(BF16)
        for d in range(nz):
            sent[s, ch, d] = block[d * zr : (d + 1) * zr]
        back_z[s, ch, 0] = block[:zr]
        return [
            start(("w", s, ch, d), sent.at[s, ch, d], back_z.at[s, ch, d], at(dz=-d))
            for d in range(1, nz)
        ]

    results = []

    def finish(s, ch, copies):
        for copy in copies:
            copy.wait_recv()
        block = jnp.concatenate([back_z[s, ch, d] for d in range(nz)], axis=0)
        picked = dot(unselect[...], block)
        staging, out = ((tokens, outputs), (cotangent, input_grad))[s]
        cols = pl.ds(ch * wide, wide)
        staging[:, cols] = (picked if s else weight * picked).astype(BF16)
        if ch == CHUNKS - 1:
            result = pltpu.make_async_copy(staging, out, local_sem.at[s])
            result.start()
            results.append(result)

    def up_tile(ch):
        cols = pl.ds(ch * wide, wide)
        up[cols, :] = dot(routed[0, ch], hidden_grad[...], ((0,), (0,))).astype(BF16)

    def down_tile(ch):
        cols = pl.ds(ch * wide, wide)
        down[:, cols] = dot(hidden[...], routed[1, ch], ((0,), (0,))).astype(BF16)

    def write(buffer, out, number):
        result = pltpu.make_async_copy(buffer, out, local_sem.at[number])
        result.start()
        results.append(result)

    pick(0)
    pl.semaphore_wait(barrier, len(peers))
    z_t = send_z(0)
    swaps = [
        start(("s", i), own, buffer, at(dx=1 + 2 * x_lo))
        for i, (own, buffer) in enumerate(((up_in, up), (down_in, down)))
    ]
    pick(1)
    z_g = send_z(1)
    y_t = to_ring_y(0, z_t)
    to_ring_x(0, y_t)
    x_t = send_x(0)
    y_g = to_ring_y(1, z_g)
    to_ring_x(1, y_g)
    x_g = send_x(1)
    shared_t = share(0, x_t)
    take_weights(swaps)
    settle(y_t + [x_t[1], x_t[3]])
    forward(shared_t)
    p_t = [parts(0, ch) for ch in range(CHUNKS)]
    b_t, v_t, w_t, b_g, v_g, w_g = {}, {}, {}, {}, {}, {}
    b_t[0] = chip_sum(0, 0, p_t[0])
    b_t[1] = chip_sum(0, 1, p_t[1])
    shared_g = share(1, x_g)
    settle(y_g + [x_g[1], x_g[3]])
    backward(shared_g)
    p_g = [parts(1, 0)]
    v_t[0] = from_ring_x(0, 0, b_t[0])
    b_t[2] = chip_sum(0, 2, p_t[2])
    p_g.append(parts(1, 1))
    v_t[1] = from_ring_x(0, 1, b_t[1])
    b_t[3] = chip_sum(0, 3, p_t[3])
    settle(z_t + z_g)
    w_t[0] = from_ring_y(0, 0, v_t[0])
    p_g.append(parts(1, 2))
    b_g[0] = chip_sum(1, 0, p_g[0])
    v_t[2] = from_ring_x(0, 2, b_t[2])
    w_t[1] = from_ring_y(0, 1, v_t[1])
    p_g.append(parts(1, 3))
    b_g[1] = chip_sum(1, 1, p_g[1])
    v_t[3] = from_ring_x(0, 3, b_t[3])
    w_t[2] = from_ring_y(0, 2, v_t[2])
    b_g[2] = chip_sum(1, 2, p_g[2])
    for ch in range(2):
        up_tile(ch)
    v_g[0] = from_ring_x(1, 0, b_g[0])
    w_t[3] = from_ring_y(0, 3, v_t[3])
    b_g[3] = chip_sum(1, 3, p_g[3])
    for ch in range(2, CHUNKS):
        up_tile(ch)
    write(up, up_grad, 2)
    v_g[1] = from_ring_x(1, 1, b_g[1])
    w_g[0] = from_ring_y(1, 0, v_g[0])
    finish(0, 0, w_t[0])
    for ch in range(2):
        down_tile(ch)
    v_g[2] = from_ring_x(1, 2, b_g[2])
    w_g[1] = from_ring_y(1, 1, v_g[1])
    finish(0, 1, w_t[1])
    for ch in range(2, CHUNKS):
        down_tile(ch)
    write(down, down_grad, 3)
    v_g[3] = from_ring_x(1, 3, b_g[3])
    w_g[2] = from_ring_y(1, 2, v_g[2])
    finish(0, 2, w_t[2])
    w_g[3] = from_ring_y(1, 3, v_g[3])
    finish(0, 3, w_t[3])
    for ch in range(CHUNKS):
        finish(1, ch, w_g[ch])
    settle(list(waiting.values()))
    for result in results:
        result.wait()


def shards(geo, tokens, cotangent, routes, router_probs, up_weight, down_weight, moving):
    ny, nz = geo.ny, geo.nz
    count, width = tokens.shape
    hid = up_weight.shape[2]
    rows, xr, wide = geo.rows, geo.xrows, width // CHUNKS
    vmem = pl.BlockSpec(memory_space=pltpu.VMEM)
    smem = pl.BlockSpec(memory_space=pltpu.SMEM)
    anywhere = pl.BlockSpec(memory_space=pl.ANY)
    copies = 2 * (nz - 1 + ny - 1 + 3 + 4 + CHUNKS * (1 + 3 + ny - 1 + nz - 1)) + 2
    buffer = lambda *shape: pltpu.VMEM(shape, BF16)
    outputs, input_grad, up_grad, down_grad = pl.pallas_call(
        functools.partial(kernel, geo),
        out_shape=(
            jax.ShapeDtypeStruct((count, width), BF16),
            jax.ShapeDtypeStruct((count, width), BF16),
            jax.ShapeDtypeStruct((width, hid), BF16),
            jax.ShapeDtypeStruct((hid, width), BF16),
        ),
        in_specs=[anywhere, anywhere, vmem, vmem, smem, anywhere, anywhere] + [vmem] * 4,
        out_specs=(anywhere,) * 4,
        scratch_shapes=[
            buffer(count, width),
            buffer(count, width),
            buffer(width, hid),
            buffer(hid, width),
            buffer(width, hid),
            buffer(hid, width),
            buffer(8 * xr, hid),
            buffer(8 * xr, hid),
            pltpu.VMEM((8 * xr, hid), F32),
            buffer(rows, count),
            buffer(count, rows),
            buffer(2, CHUNKS, nz, geo.zrows, wide),
            buffer(2, CHUNKS, nz, geo.zrows, wide),
            buffer(2, CHUNKS, rows, wide),
            buffer(2, CHUNKS, 8 * xr, wide),
            buffer(2, CHUNKS, 8 * xr, wide),
            buffer(2, CHUNKS, 4 * xr, wide),
            buffer(2, CHUNKS, 3 * xr, wide),
            buffer(2, CHUNKS, rows, wide),
            buffer(2, CHUNKS, nz, geo.zrows, wide),
            pltpu.SemaphoreType.DMA((copies,)),
            pltpu.SemaphoreType.DMA((copies,)),
            pltpu.SemaphoreType.DMA((4,)),
        ],
        compiler_params=pltpu.CompilerParams(
            collective_id=0, has_side_effects=True, vmem_limit_bytes=63 * 2**20
        ),
    )(
        tokens,
        cotangent,
        routes.reshape(1, count),
        router_probs.reshape(1, count),
        moving,
        up_weight[0],
        down_weight[0],
        *[jnp.asarray(m) for m in geo.matrices()],
    )
    return outputs, input_grad, up_grad[None], down_grad[None]


def solution(mesh):
    ep_count = mesh.shape["ep"]
    nz = 8 if ep_count == 64 else 2
    geo = Geometry(ep_count // 2 // nz, nz)
    in_specs = (
        P(("ep", "dp"), None),
        P(("ep", "dp"), None),
        P(("ep", "dp"), None),
        P(("ep", "dp"), None),
        P("ep", None, "dp"),
        P("ep", "dp", None),
        P(),
    )
    out_specs = (
        P(("ep", "dp"), None),
        P(("ep", "dp"), None),
        P("ep", None, "dp"),
        P("ep", "dp", None),
    )
    return jax.shard_map(
        functools.partial(shards, geo),
        mesh=mesh,
        in_specs=in_specs,
        out_specs=out_specs,
        check_vma=False,
    )
```

```python
import functools

import jax
import jax.numpy as jnp
import numpy as np
from jax import lax
from jax.experimental import pallas as pl
from jax.experimental.pallas import tpu as pltpu
from jax.sharding import PartitionSpec as P

MESH = pl.DeviceIdType.MESH
NX = 4
CAP = 3
CHUNKS = 7
LEAD = 2
TILES = 3
SPANS = ((0, 4), (4, 3))
PIECES = 4
BF16 = jnp.bfloat16
F32 = jnp.float32
I32 = jnp.int32


def dot(left, right, dims=((1,), (0,))):
    return lax.dot_general(left, right, (dims, ((), ())), preferred_element_type=F32)


def loop(count, body):
    def run(i, _):
        body(i)
        return 0

    lax.fori_loop(0, count, run, 0)


class Geometry:
    def __init__(self, ny, nz):
        self.ny, self.nz = ny, nz
        self.zrows = ny * 2 * CAP
        self.yrows = 2 * nz * CAP
        self.xrows = ny * nz * CAP
        self.rows = 2 * self.xrows

    def matrices(self):
        ny, nz, rows = self.ny, self.nz, self.rows
        by_z = np.arange(rows).reshape(nz, ny, 2, CAP)
        by_y = np.arange(rows).reshape(ny, 2, nz, CAP)
        to_y = np.zeros((rows, rows), np.float32)
        to_y[np.arange(rows), by_z.transpose(1, 2, 0, 3).reshape(-1)] = 1
        to_x = np.zeros((rows, rows), np.float32)
        to_x[np.arange(rows), by_y.transpose(1, 0, 2, 3).reshape(-1)] = 1
        return [m.astype(jnp.bfloat16) for m in (to_y, to_y.T, to_x, to_x.T)]


def kernel(
    geo,
    tokens_in,
    cotangent_in,
    routes,
    probs,
    moving,
    up_in,
    down_in,
    to_y,
    from_y,
    to_x,
    from_x,
    outputs,
    input_grad,
    up_grad,
    down_grad,
    tokens,
    cotangent,
    up_own,
    down_own,
    up,
    down,
    hidden_grad,
    hidden,
    slope,
    their_hidden,
    their_grad,
    select,
    unselect,
    sent,
    got_z,
    got_y,
    routed,
    part,
    core_part,
    x_part,
    back_y,
    back_z,
    send_sem,
    recv_sem,
    local_sem,
):
    ny, nz = geo.ny, geo.nz
    xr, yr, zr, rows = geo.xrows, geo.yrows, geo.zrows, geo.rows
    count, width = tokens.shape
    wide = width // CHUNKS
    ep, dp = lax.axis_index("ep"), lax.axis_index("dp")
    x_lo, y, z = ep // (ny * nz), (ep // nz) % ny, ep % nz
    x, core = (dp // 2) * 2 + x_lo, dp % 2

    def at(dx=0, dy=0, dz=0, dc=0):
        nx_, ny_, nz_ = (x + dx) % NX, (y + dy % ny) % ny, (z + dz % nz) % nz
        return ((nx_ % 2) * (ny * nz) + ny_ * nz + nz_, (nx_ // 2) * 2 + (core + dc) % 2)

    peers = (
        [at(dz=d) for d in range(1, nz)]
        + [at(dy=d) for d in range(1, ny)]
        + [at(dx=d) for d in range(1, NX)]
        + [at(dc=1)]
    )
    barrier = pltpu.get_barrier_semaphore()
    for peer in peers:
        pl.semaphore_signal(barrier, inc=1, device_id=peer, device_id_type=MESH)

    loads = [
        pltpu.make_async_copy(src, dst, local_sem.at[i])
        for i, (src, dst) in enumerate(
            (
                (tokens_in, tokens),
                (cotangent_in, cotangent),
                (up_in, up_own),
                (down_in, down_own),
            )
        )
    ]
    for load in loads:
        load.start()

    used = {}
    waiting = {}

    def start(key, src, dst, device):
        number = used.setdefault(key, len(used))
        copy = pltpu.make_async_remote_copy(
            src_ref=src,
            dst_ref=dst,
            send_sem=send_sem.at[number],
            recv_sem=recv_sem.at[number],
            device_id=device,
            device_id_type=MESH,
        )
        copy.start()
        waiting[id(copy)] = copy
        return copy

    def settle(copies):
        for copy in copies:
            copy.wait_send()
            del waiting[id(copy)]

    def y_block(d):
        return pl.ds(d * yr, yr)

    def x_block(d):
        return pl.ds(d * xr, xr)

    def chunk_cols(ch):
        return pl.ds(pl.multiple_of(ch * wide, wide), wide)

    half_count = ny * nz
    expert = routes[...]
    flip = jnp.zeros_like(expert)
    for pair in range(half_count):
        flip += jnp.where((expert & (half_count - 1)) == pair, moving[pair], 0)
    target_row = (expert + half_count * flip) & (2 * half_count - 1)
    down_iota = lax.broadcasted_iota(I32, (count, count), 0)
    across_iota = lax.broadcasted_iota(I32, (count, count), 1)

    def as_column(row):
        spread = jnp.where(down_iota == across_iota, row.astype(F32), 0.0)
        return jnp.sum(spread, axis=1, keepdims=True)

    target_column = as_column(target_row).astype(I32)
    same = target_column == target_row
    rank_row = jnp.sum(
        jnp.where(same & (down_iota < across_iota), 1.0, 0.0), axis=0, keepdims=True
    ).astype(I32)

    def slot_of(target, rank):
        dz = (target - z) & (nz - 1)
        dy = (target // nz - y) & (ny - 1)
        cross = (target // half_count) ^ x_lo
        return dz * zr + (dy * 2 + cross) * CAP + rank

    slot_row = slot_of(target_row, rank_row)
    slot_column = as_column(slot_row).astype(I32)
    select[...] = jnp.where(
        lax.broadcasted_iota(I32, (rows, count), 0) == slot_row, 1.0, 0.0
    ).astype(BF16)
    unselect[...] = jnp.where(
        lax.broadcasted_iota(I32, (count, rows), 1) == slot_column, 1.0, 0.0
    ).astype(BF16)
    weight = as_column(probs[...])

    def pick(s, first, number):
        def tile(i):
            ch = first + i
            cols = chunk_cols(ch)
            if s == 0:
                given = tokens[:, cols]
            else:
                given = (weight * cotangent[:, cols].astype(F32)).astype(BF16)
            block = dot(select[...], given).astype(BF16)
            for d in range(nz):
                sent[s, ch, d] = block[d * zr : (d + 1) * zr]
            got_z[s, ch, 0] = block[:zr]

        loop(number, tile)
        span = pl.ds(first, number)
        return [
            start(("z", s, first, d), sent.at[s, span, d], got_z.at[s, span, d], at(dz=d))
            for d in range(1, nz)
        ]

    def to_ring_y(s, first, number, copies):
        for copy in copies:
            copy.wait_recv()

        def tile(i):
            ch = first + i
            block = jnp.concatenate([got_z[s, ch, d] for d in range(nz)], axis=0)
            block = dot(to_y[...], block).astype(BF16)
            part[s, ch, pl.ds(0, rows), :] = block
            got_y[s, ch, y_block(0), :] = block[:yr]

        loop(number, tile)
        span = pl.ds(first, number)
        return [
            start(
                ("y", s, first, d),
                part.at[s, span, y_block(d)],
                got_y.at[s, span, y_block(d)],
                at(dy=d),
            )
            for d in range(1, ny)
        ]

    def to_ring_x(s, first, number, copies):
        for copy in copies:
            copy.wait_recv()

        def tile(i):
            ch = first + i
            block = dot(to_x[...], got_y[s, ch]).astype(BF16)
            routed[s, ch, x_block(0), :] = block[:xr]
            part[s, ch, pl.ds(rows, xr), :] = block[xr:]

        loop(number, tile)
        span = pl.ds(first, number)
        other = part.at[s, span, pl.ds(rows, xr)]
        own = routed.at[s, span, x_block(0)]
        return {
            1: start(("x", s, first, 1), other, routed.at[s, span, x_block(1)], at(dx=1)),
            3: start(("x", s, first, 3), other, routed.at[s, span, x_block(3)], at(dx=3)),
            2: start(("x", s, first, 2), own, routed.at[s, span, x_block(2)], at(dx=2)),
            0: start(("c", s, first, 0), own, routed.at[s, span, x_block(4)], at(dc=1)),
        }

    def share(s, first, number, made):
        shared = [made[0]]
        span = pl.ds(first, number)
        for d in (1, 3, 2):
            made[d].wait_recv()
            shared.append(
                start(
                    ("c", s, first, d),
                    routed.at[s, span, x_block(d)],
                    routed.at[s, span, x_block(4 + d)],
                    at(dc=1),
                )
            )
        return shared

    chosen = moving[ep % half_count] == 1

    def take_weights(swaps):
        for copy, load, buffer, own, parts in zip(
            swaps, loads[2:], (up, down), (up_own, down_own), (7, 4)
        ):
            load.wait()
            copy.wait_recv()
            step = buffer.shape[0] // parts

            def run(i, buffer=buffer, own=own, step=step):
                at_rows = pl.ds(pl.multiple_of(i * step, step), step)
                buffer[at_rows, :] = lax.select(chosen, buffer[at_rows, :], own[at_rows, :])

            loop(parts, run)

    def group(i):
        return pl.ds(pl.multiple_of(i * 4 * xr, 4 * xr), 4 * xr)

    def forward(shared):
        for copy in shared:
            copy.wait_recv()

        def run(i):
            value = dot(routed[0, 0, group(i), :], up[pl.ds(0, wide), :])
            for ch in range(1, CHUNKS):
                value += dot(routed[0, ch, group(i), :], up[pl.ds(ch * wide, wide), :])
            sigmoid = jax.nn.sigmoid(value)
            hidden[group(i), :] = (value * sigmoid).astype(BF16)
            slope[group(i), :] = sigmoid * (1.0 + value * (1.0 - sigmoid))

        loop(2, run)

    def backward(shared):
        for copy in shared:
            copy.wait_recv()
        over_cols = ((1,), (1,))

        def run(i):
            value = dot(routed[1, 0, group(i), :], down[:, pl.ds(0, wide)], over_cols)
            for ch in range(1, CHUNKS):
                cols = pl.ds(ch * wide, wide)
                value += dot(routed[1, ch, group(i), :], down[:, cols], over_cols)
            hidden_grad[group(i), :] = (value * slope[group(i), :]).astype(BF16)

        loop(2, run)

    def traded(s):
        mine, theirs = ((hidden, their_hidden), (hidden_grad, their_grad))[s]
        copies = []
        for block, other in ((0, 2), (2, 0), (4, 6), (6, 4)):
            number = used.setdefault(("t", s, block), len(used))
            copies.append(
                pltpu.make_async_remote_copy(
                    src_ref=mine.at[pl.ds(block * xr, 2 * xr)],
                    dst_ref=theirs.at[pl.ds(other * xr, 2 * xr)],
                    send_sem=send_sem.at[number],
                    recv_sem=recv_sem.at[number],
                    device_id=at(dx=2),
                    device_id_type=MESH,
                )
            )
        return copies

    def trade(s):
        @pl.when(core == 1)
        def _():
            for copy in traded(s):
                copy.start()

    def take_traded(s):
        mine, theirs = ((hidden, their_hidden), (hidden_grad, their_grad))[s]

        @pl.when(core == 1)
        def _():
            for copy in traded(s):
                copy.wait()

            def run(i):
                mine[group(i), :] = lax.select(chosen, theirs[group(i), :], mine[group(i), :])

            loop(2, run)

    def parts(s, ch):
        def run(i):
            if s == 0:
                block = dot(hidden[group(i), :], down[:, pl.ds(ch * wide, wide)])
            else:
                block = dot(
                    hidden_grad[group(i), :], up[pl.ds(ch * wide, wide), :], ((1,), (1,))
                )
            part[s, ch, group(i), :] = block.astype(BF16)

        loop(2, run)
        far = part.at[s, ch, pl.ds(4 * xr, 4 * xr)]
        return start(("p", s, ch), far, core_part.at[s, ch], at(dc=1))

    def chip_sum(s, ch, copy):
        copy.wait_recv()

        def run(i):
            block = x_block_at(i)
            total = part[s, ch, block, :].astype(F32) + core_part[s, ch, block, :].astype(F32)
            part[s, ch, block, :] = total.astype(BF16)

        loop(4, run)
        return [
            start(
                ("b", s, ch, d),
                part.at[s, ch, x_block(d)],
                x_part.at[s, ch, x_block(place)],
                at(dx=NX - d),
            )
            for d, place in ((1, 1), (3, 2), (2, 0))
        ]

    def x_block_at(i):
        return pl.ds(pl.multiple_of(i * xr, xr), xr)

    def from_ring_x(s, ch, copies):
        for copy in copies:
            copy.wait_recv()
        taken = [x_part[s, ch, x_block(i), :].astype(F32) for i in range(3)]
        same_x = (part[s, ch, x_block(0), :].astype(F32) + taken[0]).astype(BF16)
        cross_x = (taken[1] + taken[2]).astype(BF16)
        block = dot(from_x[...], jnp.concatenate([same_x, cross_x], axis=0)).astype(BF16)
        got_y[s, ch] = block
        back_y[s, ch, y_block(0), :] = block[:yr]
        return [
            start(
                ("v", s, ch, d),
                got_y.at[s, ch, y_block(d)],
                back_y.at[s, ch, y_block(d)],
                at(dy=-d),
            )
            for d in range(1, ny)
        ]

    def from_ring_y(s, ch, copies):
        for copy in copies:
            copy.wait_recv()
        block = dot(from_y[...], back_y[s, ch]).astype(BF16)
        for d in range(nz):
            sent[s, ch, d] = block[d * zr : (d + 1) * zr]
        back_z[s, ch, 0] = block[:zr]
        return [
            start(("w", s, ch, d), sent.at[s, ch, d], back_z.at[s, ch, d], at(dz=-d))
            for d in range(1, nz)
        ]

    results = []

    def finish(s, ch, copies):
        for copy in copies:
            copy.wait_recv()
        block = jnp.concatenate([back_z[s, ch, d] for d in range(nz)], axis=0)
        picked = dot(unselect[...], block)
        staging, out = ((tokens, outputs), (cotangent, input_grad))[s]
        cols = pl.ds(ch * wide, wide)
        staging[:, cols] = (picked if s else weight * picked).astype(BF16)
        if ch == CHUNKS - 1:
            result = pltpu.make_async_copy(staging, out, local_sem.at[s])
            result.start()
            results.append(result)

    def up_tile(ch):
        cols = pl.ds(ch * wide, wide)
        up[cols, :] = dot(routed[0, ch], hidden_grad[...], ((0,), (0,))).astype(BF16)

    def down_tile(ch):
        cols = pl.ds(ch * wide, wide)
        down[:, cols] = dot(hidden[...], routed[1, ch], ((0,), (0,))).astype(BF16)

    def write(buffer, out, number):
        result = pltpu.make_async_copy(buffer, out, local_sem.at[number])
        result.start()
        results.append(result)

    pl.semaphore_wait(barrier, len(peers))
    swaps = [
        start(("s", i), own, buffer, at(dx=1 + 2 * (x_lo ^ core)))
        for i, (own, buffer) in enumerate(((up_in, up), (down_in, down)))
    ]
    streams = [(s, *span) for s in range(2) for span in SPANS]
    along_z, along_y, along_x, shared = [], [], [], ([], [])
    for s, first, number in streams:
        if first == 0:
            loads[s].wait()
        along_z.append(pick(s, first, number))
    for stream, copies in zip(streams, along_z):
        along_y.append(to_ring_y(*stream, copies))
        along_x.append(to_ring_x(*stream, along_y[-1]))
        done = len(along_x) - 3
        if done >= 0:
            shared[0].extend(share(*streams[done], along_x[done]))
    from_part = [along_y[i] + [along_x[i][1], along_x[i][3]] for i in range(4)]
    take_weights(swaps)
    settle(from_part[0] + from_part[1])
    forward(shared[0])
    trade(0)
    part_sent = [parts(0, ch) for ch in range(CHUNKS)]
    items = [(s, ch) for s in range(2) for ch in range(CHUNKS)]
    x_given, y_given, z_given = {}, {}, {}
    for i in range(LEAD):
        x_given[i] = chip_sum(*items[i], part_sent[i])
    for done in (2, 3):
        shared[1].extend(share(*streams[done], along_x[done]))
    settle(from_part[2] + from_part[3])
    backward(shared[1])
    trade(1)
    for copies in along_z:
        settle(copies)
    tiles = [functools.partial(take_traded, 1)]
    tiles += [functools.partial(up_tile, ch) for ch in range(CHUNKS)]
    tiles += [lambda: write(up, up_grad, 2), functools.partial(take_traded, 0)]
    tiles += [functools.partial(down_tile, ch) for ch in range(CHUNKS)]
    tiles.append(lambda: write(down, down_grad, 3))
    for i in range(LEAD, len(items) + LEAD + 4):
        x_done, y_done, z_done = i - LEAD, i - LEAD - 1, i - LEAD - 4
        if x_done in x_given:
            y_given[x_done] = from_ring_x(*items[x_done], x_given[x_done])
        if i < len(items):
            x_given[i] = chip_sum(*items[i], part_sent[i])
        if i - LEAD < CHUNKS:
            part_sent.append(parts(1, i - LEAD))
        if y_done in y_given:
            z_given[y_done] = from_ring_y(*items[y_done], y_given[y_done])
        if i - LEAD >= CHUNKS - 1:
            for _ in range(min(TILES, len(tiles))):
                tiles.pop(0)()
        if z_done in z_given:
            finish(*items[z_done], z_given[z_done])
    settle(list(waiting.values()))
    for result in results:
        result.wait()


def place(*refs):
    sources, targets, held, into, out_of = refs[:4], refs[4:8], refs[8:12], refs[12], refs[13]
    loads, stores = [], []
    for i in range(4):
        step = sources[i].shape[0] // PIECES
        for j in range(PIECES):
            rows, number = pl.ds(j * step, step), PIECES * i + j
            source, target, own = (ref[i].at[rows] for ref in (sources, targets, held))
            loads.append(pltpu.make_async_copy(source, own, into.at[number]))
            stores.append(pltpu.make_async_copy(own, target, out_of.at[number]))
            loads[-1].start()
    for load, store in zip(loads, stores):
        load.wait()
        store.start()
    for store in stores:
        store.wait()


def shards(geo, tokens, cotangent, routes, router_probs, up_weight, down_weight, moving):
    ny, nz = geo.ny, geo.nz
    count, width = tokens.shape
    hid = up_weight.shape[2]
    rows, xr, wide = geo.rows, geo.xrows, width // CHUNKS
    vmem = pl.BlockSpec(memory_space=pltpu.VMEM)
    smem = pl.BlockSpec(memory_space=pltpu.SMEM)
    anywhere = pl.BlockSpec(memory_space=pl.ANY)
    out_copies = len(SPANS) * (nz - 1 + ny - 1 + 3 + 4)
    copies = 2 * (out_copies + CHUNKS * (1 + 3 + ny - 1 + nz - 1) + 4) + 2
    buffer = lambda *shape: pltpu.VMEM(shape, BF16)
    results = pl.pallas_call(
        functools.partial(kernel, geo),
        out_shape=(
            jax.ShapeDtypeStruct((count, width), BF16),
            jax.ShapeDtypeStruct((count, width), BF16),
            jax.ShapeDtypeStruct((width, hid), BF16),
            jax.ShapeDtypeStruct((hid, width), BF16),
        ),
        in_specs=[anywhere, anywhere, vmem, vmem, smem, anywhere, anywhere] + [vmem] * 4,
        out_specs=(anywhere,) * 4,
        scratch_shapes=[
            buffer(count, width),
            buffer(count, width),
            buffer(width, hid),
            buffer(hid, width),
            buffer(width, hid),
            buffer(hid, width),
            buffer(8 * xr, hid),
            buffer(8 * xr, hid),
            pltpu.VMEM((8 * xr, hid), F32),
            buffer(8 * xr, hid),
            buffer(8 * xr, hid),
            buffer(rows, count),
            buffer(count, rows),
            buffer(2, CHUNKS, nz, geo.zrows, wide),
            buffer(2, CHUNKS, nz, geo.zrows, wide),
            buffer(2, CHUNKS, rows, wide),
            buffer(2, CHUNKS, 8 * xr, wide),
            buffer(2, CHUNKS, 8 * xr, wide),
            buffer(2, CHUNKS, 4 * xr, wide),
            buffer(2, CHUNKS, 3 * xr, wide),
            buffer(2, CHUNKS, rows, wide),
            buffer(2, CHUNKS, nz, geo.zrows, wide),
            pltpu.SemaphoreType.DMA((copies,)),
            pltpu.SemaphoreType.DMA((copies,)),
            pltpu.SemaphoreType.DMA((4,)),
        ],
        compiler_params=pltpu.CompilerParams(
            collective_id=0, has_side_effects=True, vmem_limit_bytes=63 * 2**20
        ),
    )(
        tokens,
        cotangent,
        routes.reshape(1, count),
        router_probs.reshape(1, count),
        moving,
        up_weight[0],
        down_weight[0],
        *[jnp.asarray(m) for m in geo.matrices()],
    )
    outputs, input_grad, up_grad, down_grad = pl.pallas_call(
        place,
        out_shape=[jax.ShapeDtypeStruct(r.shape, r.dtype) for r in results],
        in_specs=[anywhere] * 4,
        out_specs=[anywhere] * 4,
        scratch_shapes=[pltpu.VMEM(r.shape, r.dtype) for r in results]
        + [pltpu.SemaphoreType.DMA((4 * PIECES,))] * 2,
    )(*results)
    return outputs, input_grad, up_grad[None], down_grad[None]


def solution(mesh):
    ep_count = mesh.shape["ep"]
    nz = 8 if ep_count == 64 else 2
    geo = Geometry(ep_count // 2 // nz, nz)
    in_specs = (
        P(("ep", "dp"), None),
        P(("ep", "dp"), None),
        P(("ep", "dp"), None),
        P(("ep", "dp"), None),
        P("ep", None, "dp"),
        P("ep", "dp", None),
        P(),
    )
    out_specs = (
        P(("ep", "dp"), None),
        P(("ep", "dp"), None),
        P("ep", None, "dp"),
        P("ep", "dp", None),
    )
    return jax.shard_map(
        functools.partial(shards, geo),
        mesh=mesh,
        in_specs=in_specs,
        out_specs=out_specs,
        check_vma=False,
    )
```

```python
import functools

import jax
import jax.numpy as jnp
import numpy as np
from jax import lax
from jax.experimental import pallas as pl
from jax.experimental.pallas import tpu as pltpu
from jax.sharding import PartitionSpec as P

MESH = pl.DeviceIdType.MESH
NX = 4
CAP = 3
CHUNKS = 7
LEAD = 2
TILES = 3
SPANS = ((0, 2), (2, 5))
PIECES = 2
VMEM_LIMIT = 57 * 2**20
BF16 = jnp.bfloat16
F32 = jnp.float32
I32 = jnp.int32


def dot(left, right, dims=((1,), (0,))):
    return lax.dot_general(left, right, (dims, ((), ())), preferred_element_type=F32)


def loop(count, body):
    def run(i, _):
        body(i)
        return 0

    lax.fori_loop(0, count, run, 0)


class Geometry:
    def __init__(self, ny, nz):
        self.ny, self.nz = ny, nz
        self.zrows = ny * 2 * CAP
        self.yrows = 2 * nz * CAP
        self.xrows = ny * nz * CAP
        self.rows = 2 * self.xrows

    def matrices(self):
        ny, nz, rows = self.ny, self.nz, self.rows
        by_z = np.arange(rows).reshape(nz, ny, 2, CAP)
        by_y = np.arange(rows).reshape(ny, 2, nz, CAP)
        to_y = np.zeros((rows, rows), np.float32)
        to_y[np.arange(rows), by_z.transpose(1, 2, 0, 3).reshape(-1)] = 1
        to_x = np.zeros((rows, rows), np.float32)
        to_x[np.arange(rows), by_y.transpose(1, 0, 2, 3).reshape(-1)] = 1
        return [m.astype(jnp.bfloat16) for m in (to_y, to_y.T, to_x, to_x.T)]


def kernel(
    geo,
    tokens_in,
    cotangent_in,
    routes,
    probs,
    moving,
    up_in,
    down_in,
    to_y,
    from_y,
    to_x,
    from_x,
    tokens,
    cotangent,
    up,
    down,
    up_own,
    down_own,
    hidden_grad,
    hidden,
    slope,
    their_hidden,
    their_grad,
    select,
    unselect,
    sent,
    got_z,
    got_y,
    routed,
    part,
    core_part,
    x_part,
    back_y,
    back_z,
    send_sem,
    recv_sem,
    local_sem,
):
    ny, nz = geo.ny, geo.nz
    xr, yr, zr, rows = geo.xrows, geo.yrows, geo.zrows, geo.rows
    count, width = tokens.shape
    wide = width // CHUNKS
    ep, dp = lax.axis_index("ep"), lax.axis_index("dp")
    x_lo, y, z = ep // (ny * nz), (ep // nz) % ny, ep % nz
    x, core = (dp // 2) * 2 + x_lo, dp % 2

    def at(dx=0, dy=0, dz=0, dc=0):
        nx_, ny_, nz_ = (x + dx) % NX, (y + dy % ny) % ny, (z + dz % nz) % nz
        return ((nx_ % 2) * (ny * nz) + ny_ * nz + nz_, (nx_ // 2) * 2 + (core + dc) % 2)

    peers = (
        [at(dz=d) for d in range(1, nz)]
        + [at(dy=d) for d in range(1, ny)]
        + [at(dx=d) for d in range(1, NX)]
        + [at(dc=1)]
    )
    barrier = pltpu.get_barrier_semaphore()
    for peer in peers:
        pl.semaphore_signal(barrier, inc=1, device_id=peer, device_id_type=MESH)

    loads = [
        pltpu.make_async_copy(src, dst, local_sem.at[i])
        for i, (src, dst) in enumerate(
            (
                (tokens_in, tokens),
                (cotangent_in, cotangent),
                (up_in, up_own),
                (down_in, down_own),
            )
        )
    ]
    for load in loads:
        load.start()

    used = {}
    waiting = {}

    def start(key, src, dst, device):
        number = used.setdefault(key, len(used))
        copy = pltpu.make_async_remote_copy(
            src_ref=src,
            dst_ref=dst,
            send_sem=send_sem.at[number],
            recv_sem=recv_sem.at[number],
            device_id=device,
            device_id_type=MESH,
        )
        copy.start()
        waiting[id(copy)] = copy
        return copy

    def settle(copies):
        for copy in copies:
            copy.wait_send()
            del waiting[id(copy)]

    def y_block(d):
        return pl.ds(d * yr, yr)

    def x_block(d):
        return pl.ds(d * xr, xr)

    def chunk_cols(ch):
        return pl.ds(pl.multiple_of(ch * wide, wide), wide)

    half_count = ny * nz
    expert = routes[...]
    flip = jnp.zeros_like(expert)
    for pair in range(half_count):
        flip += jnp.where((expert & (half_count - 1)) == pair, moving[pair], 0)
    target_row = (expert + half_count * flip) & (2 * half_count - 1)
    down_iota = lax.broadcasted_iota(I32, (count, count), 0)
    across_iota = lax.broadcasted_iota(I32, (count, count), 1)

    def as_column(row):
        spread = jnp.where(down_iota == across_iota, row.astype(F32), 0.0)
        return jnp.sum(spread, axis=1, keepdims=True)

    target_column = as_column(target_row).astype(I32)
    same = target_column == target_row
    rank_row = jnp.sum(
        jnp.where(same & (down_iota < across_iota), 1.0, 0.0), axis=0, keepdims=True
    ).astype(I32)

    def slot_of(target, rank):
        dz = (target - z) & (nz - 1)
        dy = (target // nz - y) & (ny - 1)
        cross = (target // half_count) ^ x_lo
        return dz * zr + (dy * 2 + cross) * CAP + rank

    slot_row = slot_of(target_row, rank_row)
    slot_column = as_column(slot_row).astype(I32)
    select[...] = jnp.where(
        lax.broadcasted_iota(I32, (rows, count), 0) == slot_row, 1.0, 0.0
    ).astype(BF16)
    unselect[...] = jnp.where(
        lax.broadcasted_iota(I32, (count, rows), 1) == slot_column, 1.0, 0.0
    ).astype(BF16)
    weight = as_column(probs[...])

    def pick(s, first, number):
        def tile(i):
            ch = first + i
            cols = chunk_cols(ch)
            if s == 0:
                given = tokens[:, cols]
            else:
                given = (weight * cotangent[:, cols].astype(F32)).astype(BF16)
            block = dot(select[...], given).astype(BF16)
            for d in range(nz):
                sent[s, ch, d] = block[d * zr : (d + 1) * zr]
            got_z[s, ch, 0] = block[:zr]

        loop(number, tile)
        span = pl.ds(first, number)
        return [
            start(("z", s, first, d), sent.at[s, span, d], got_z.at[s, span, d], at(dz=d))
            for d in range(1, nz)
        ]

    def to_ring_y(s, first, number, copies):
        for copy in copies:
            copy.wait_recv()

        def tile(i):
            ch = first + i
            block = jnp.concatenate([got_z[s, ch, d] for d in range(nz)], axis=0)
            block = dot(to_y[...], block).astype(BF16)
            part[s, ch, pl.ds(0, rows), :] = block
            got_y[s, ch, y_block(0), :] = block[:yr]

        loop(number, tile)
        span = pl.ds(first, number)
        return [
            start(
                ("y", s, first, d),
                part.at[s, span, y_block(d)],
                got_y.at[s, span, y_block(d)],
                at(dy=d),
            )
            for d in range(1, ny)
        ]

    def to_ring_x(s, first, number, copies):
        for copy in copies:
            copy.wait_recv()

        def tile(i):
            ch = first + i
            block = dot(to_x[...], got_y[s, ch]).astype(BF16)
            routed[s, ch, x_block(0), :] = block[:xr]
            part[s, ch, pl.ds(rows, xr), :] = block[xr:]

        loop(number, tile)
        span = pl.ds(first, number)
        other = part.at[s, span, pl.ds(rows, xr)]
        own = routed.at[s, span, x_block(0)]
        return {
            1: start(("x", s, first, 1), other, routed.at[s, span, x_block(1)], at(dx=1)),
            3: start(("x", s, first, 3), other, routed.at[s, span, x_block(3)], at(dx=3)),
            2: start(("x", s, first, 2), own, routed.at[s, span, x_block(2)], at(dx=2)),
            0: start(("c", s, first, 0), own, routed.at[s, span, x_block(4)], at(dc=1)),
        }

    def share(s, first, number, made):
        shared = [made[0]]
        span = pl.ds(first, number)
        for d in (1, 3, 2):
            made[d].wait_recv()
            shared.append(
                start(
                    ("c", s, first, d),
                    routed.at[s, span, x_block(d)],
                    routed.at[s, span, x_block(4 + d)],
                    at(dc=1),
                )
            )
        return shared

    chosen = moving[ep % half_count] == 1

    def take_weights(swaps):
        for copy, load, buffer, own, parts in zip(
            swaps, loads[2:], (up, down), (up_own, down_own), (7, 4)
        ):
            load.wait()
            copy.wait_recv()
            step = buffer.shape[0] // parts

            def run(i, buffer=buffer, own=own, step=step):
                at_rows = pl.ds(pl.multiple_of(i * step, step), step)
                buffer[at_rows, :] = lax.select(chosen, buffer[at_rows, :], own[at_rows, :])

            loop(parts, run)

    def group(i):
        return pl.ds(pl.multiple_of(i * 4 * xr, 4 * xr), 4 * xr)

    def forward(shared):
        for copy in shared:
            copy.wait_recv()

        def run(i):
            value = dot(routed[0, 0, group(i), :], up[pl.ds(0, wide), :])
            for ch in range(1, CHUNKS):
                value += dot(routed[0, ch, group(i), :], up[pl.ds(ch * wide, wide), :])
            sigmoid = jax.nn.sigmoid(value)
            hidden[group(i), :] = (value * sigmoid).astype(BF16)
            slope[group(i), :] = sigmoid * (1.0 + value * (1.0 - sigmoid))

        loop(2, run)

    def backward(shared):
        for copy in shared:
            copy.wait_recv()
        over_cols = ((1,), (1,))

        def run(i):
            value = dot(routed[1, 0, group(i), :], down[:, pl.ds(0, wide)], over_cols)
            for ch in range(1, CHUNKS):
                cols = pl.ds(ch * wide, wide)
                value += dot(routed[1, ch, group(i), :], down[:, cols], over_cols)
            hidden_grad[group(i), :] = (value * slope[group(i), :]).astype(BF16)

        loop(2, run)

    def traded(s):
        mine, theirs = ((hidden, their_hidden), (hidden_grad, their_grad))[s]
        copies = []
        for block, other in ((0, 2), (2, 0), (4, 6), (6, 4)):
            number = used.setdefault(("t", s, block), len(used))
            copies.append(
                pltpu.make_async_remote_copy(
                    src_ref=mine.at[pl.ds(block * xr, 2 * xr)],
                    dst_ref=theirs.at[pl.ds(other * xr, 2 * xr)],
                    send_sem=send_sem.at[number],
                    recv_sem=recv_sem.at[number],
                    device_id=at(dx=2),
                    device_id_type=MESH,
                )
            )
        return copies

    def trade(s):
        @pl.when(core == 1)
        def _():
            for copy in traded(s):
                copy.start()

    def take_traded(s):
        mine, theirs = ((hidden, their_hidden), (hidden_grad, their_grad))[s]

        @pl.when(core == 1)
        def _():
            for copy in traded(s):
                copy.wait()

            def run(i):
                mine[group(i), :] = lax.select(chosen, theirs[group(i), :], mine[group(i), :])

            loop(2, run)

    def parts(s, ch):
        def run(i):
            if s == 0:
                block = dot(hidden[group(i), :], down[:, pl.ds(ch * wide, wide)])
            else:
                block = dot(
                    hidden_grad[group(i), :], up[pl.ds(ch * wide, wide), :], ((1,), (1,))
                )
            part[s, ch, group(i), :] = block.astype(BF16)

        loop(2, run)
        far = part.at[s, ch, pl.ds(4 * xr, 4 * xr)]
        return start(("p", s, ch), far, core_part.at[s, ch], at(dc=1))

    def chip_sum(s, ch, copy):
        copy.wait_recv()

        def run(i):
            block = x_block_at(i)
            total = part[s, ch, block, :].astype(F32) + core_part[s, ch, block, :].astype(F32)
            part[s, ch, block, :] = total.astype(BF16)

        loop(4, run)
        return [
            start(
                ("b", s, ch, d),
                part.at[s, ch, x_block(d)],
                x_part.at[s, ch, x_block(place)],
                at(dx=NX - d),
            )
            for d, place in ((1, 1), (3, 2), (2, 0))
        ]

    def x_block_at(i):
        return pl.ds(pl.multiple_of(i * xr, xr), xr)

    def from_ring_x(s, ch, copies):
        for copy in copies:
            copy.wait_recv()
        taken = [x_part[s, ch, x_block(i), :].astype(F32) for i in range(3)]
        same_x = (part[s, ch, x_block(0), :].astype(F32) + taken[0]).astype(BF16)
        cross_x = (taken[1] + taken[2]).astype(BF16)
        block = dot(from_x[...], jnp.concatenate([same_x, cross_x], axis=0)).astype(BF16)
        got_y[s, ch] = block
        back_y[s, ch, y_block(0), :] = block[:yr]
        return [
            start(
                ("v", s, ch, d),
                got_y.at[s, ch, y_block(d)],
                back_y.at[s, ch, y_block(d)],
                at(dy=-d),
            )
            for d in range(1, ny)
        ]

    def from_ring_y(s, ch, copies):
        for copy in copies:
            copy.wait_recv()
        block = dot(from_y[...], back_y[s, ch]).astype(BF16)
        for d in range(nz):
            sent[s, ch, d] = block[d * zr : (d + 1) * zr]
        back_z[s, ch, 0] = block[:zr]
        return [
            start(("w", s, ch, d), sent.at[s, ch, d], back_z.at[s, ch, d], at(dz=-d))
            for d in range(1, nz)
        ]

    def finish(s, ch, copies):
        for copy in copies:
            copy.wait_recv()
        block = jnp.concatenate([back_z[s, ch, d] for d in range(nz)], axis=0)
        picked = dot(unselect[...], block)
        out = (tokens, cotangent)[s]
        out[:, pl.ds(ch * wide, wide)] = (picked if s else weight * picked).astype(BF16)

    def up_tile(ch):
        cols = pl.ds(ch * wide, wide)
        up[cols, :] = dot(routed[0, ch], hidden_grad[...], ((0,), (0,))).astype(BF16)

    def down_tile(ch):
        cols = pl.ds(ch * wide, wide)
        down[:, cols] = dot(hidden[...], routed[1, ch], ((0,), (0,))).astype(BF16)

    pl.semaphore_wait(barrier, len(peers))
    swaps = [
        start(("s", i), own, buffer, at(dx=1 + 2 * (x_lo ^ core)))
        for i, (own, buffer) in enumerate(((up_in, up), (down_in, down)))
    ]
    streams = [(s, *span) for s in range(2) for span in SPANS]
    along_z, along_y, along_x, shared = [], [], [], ([], [])
    for s, first, number in streams:
        if first == 0:
            loads[s].wait()
        along_z.append(pick(s, first, number))
    for stream, copies in zip(streams, along_z):
        along_y.append(to_ring_y(*stream, copies))
        along_x.append(to_ring_x(*stream, along_y[-1]))
        done = len(along_x) - 3
        if done >= 0:
            shared[0].extend(share(*streams[done], along_x[done]))
    from_part = [along_y[i] + [along_x[i][1], along_x[i][3]] for i in range(4)]
    take_weights(swaps)
    settle(from_part[0] + from_part[1])
    forward(shared[0])
    trade(0)
    part_sent = [parts(0, ch) for ch in range(CHUNKS)]
    items = [(s, ch) for s in range(2) for ch in range(CHUNKS)]
    x_given, y_given, z_given = {}, {}, {}
    for i in range(LEAD):
        x_given[i] = chip_sum(*items[i], part_sent[i])
    for done in (2, 3):
        shared[1].extend(share(*streams[done], along_x[done]))
    settle(from_part[2] + from_part[3])
    backward(shared[1])
    trade(1)
    for copies in along_z:
        settle(copies)
    tiles = [functools.partial(take_traded, 1)]
    tiles += [functools.partial(up_tile, ch) for ch in range(CHUNKS)]
    tiles.append(functools.partial(take_traded, 0))
    tiles += [functools.partial(down_tile, ch) for ch in range(CHUNKS)]
    for i in range(LEAD, len(items) + LEAD + 4):
        x_done, y_done, z_done = i - LEAD, i - LEAD - 1, i - LEAD - 4
        if x_done in x_given:
            y_given[x_done] = from_ring_x(*items[x_done], x_given[x_done])
        if i < len(items):
            x_given[i] = chip_sum(*items[i], part_sent[i])
        if i - LEAD < CHUNKS:
            part_sent.append(parts(1, i - LEAD))
        if y_done in y_given:
            z_given[y_done] = from_ring_y(*items[y_done], y_given[y_done])
        if i - LEAD >= CHUNKS - 1:
            for _ in range(min(TILES, len(tiles))):
                tiles.pop(0)()
        if z_done in z_given:
            finish(*items[z_done], z_given[z_done])
    settle(list(waiting.values()))


def place(*refs):
    copies = []
    for i, (source, target) in enumerate(zip(refs[:4], refs[4:8])):
        step = source.shape[0] // PIECES
        for j in range(PIECES):
            rows = pl.ds(j * step, step)
            copies.append(
                pltpu.make_async_copy(
                    source.at[rows], target.at[rows], refs[8].at[PIECES * i + j]
                )
            )
            copies[-1].start()
    for copy in copies:
        copy.wait()


def shards(geo, tokens, cotangent, routes, router_probs, up_weight, down_weight, moving):
    ny, nz = geo.ny, geo.nz
    count, width = tokens.shape
    hid = up_weight.shape[2]
    rows, xr, wide = geo.rows, geo.xrows, width // CHUNKS
    vmem = pl.BlockSpec(memory_space=pltpu.VMEM)
    smem = pl.BlockSpec(memory_space=pltpu.SMEM)
    anywhere = pl.BlockSpec(memory_space=pl.ANY)
    out_copies = len(SPANS) * (nz - 1 + ny - 1 + 3 + 4)
    copies = 2 * (out_copies + CHUNKS * (1 + 3 + ny - 1 + nz - 1) + 4) + 2
    buffer = lambda *shape: pltpu.VMEM(shape, BF16)
    results = pl.pallas_call(
        functools.partial(kernel, geo),
        out_shape=(
            buffer(count, width),
            buffer(count, width),
            buffer(width, hid),
            buffer(hid, width),
        ),
        in_specs=[anywhere, anywhere, vmem, vmem, smem, anywhere, anywhere] + [vmem] * 4,
        out_specs=(vmem,) * 4,
        scratch_shapes=[
            buffer(width, hid),
            buffer(hid, width),
            buffer(8 * xr, hid),
            buffer(8 * xr, hid),
            pltpu.VMEM((8 * xr, hid), F32),
            buffer(8 * xr, hid),
            buffer(8 * xr, hid),
            buffer(rows, count),
            buffer(count, rows),
            buffer(2, CHUNKS, nz, geo.zrows, wide),
            buffer(2, CHUNKS, nz, geo.zrows, wide),
            buffer(2, CHUNKS, rows, wide),
            buffer(2, CHUNKS, 8 * xr, wide),
            buffer(2, CHUNKS, 8 * xr, wide),
            buffer(2, CHUNKS, 4 * xr, wide),
            buffer(2, CHUNKS, 3 * xr, wide),
            buffer(2, CHUNKS, rows, wide),
            buffer(2, CHUNKS, nz, geo.zrows, wide),
            pltpu.SemaphoreType.DMA((copies,)),
            pltpu.SemaphoreType.DMA((copies,)),
            pltpu.SemaphoreType.DMA((4,)),
        ],
        compiler_params=pltpu.CompilerParams(
            collective_id=0, has_side_effects=True, vmem_limit_bytes=VMEM_LIMIT
        ),
    )(
        tokens,
        cotangent,
        routes.reshape(1, count),
        router_probs.reshape(1, count),
        moving,
        up_weight[0],
        down_weight[0],
        *[jnp.asarray(m) for m in geo.matrices()],
    )
    outputs, input_grad, up_grad, down_grad = pl.pallas_call(
        place,
        out_shape=[jax.ShapeDtypeStruct(r.shape, r.dtype) for r in results],
        in_specs=[anywhere] * 4,
        out_specs=[anywhere] * 4,
        scratch_shapes=[pltpu.SemaphoreType.DMA((4 * PIECES,))],
        compiler_params=pltpu.CompilerParams(vmem_limit_bytes=2**20),
    )(*results)
    return outputs, input_grad, up_grad[None], down_grad[None]


def solution(mesh):
    ep_count = mesh.shape["ep"]
    nz = 8 if ep_count == 64 else 2
    geo = Geometry(ep_count // 2 // nz, nz)
    in_specs = (
        P(("ep", "dp"), None),
        P(("ep", "dp"), None),
        P(("ep", "dp"), None),
        P(("ep", "dp"), None),
        P("ep", None, "dp"),
        P("ep", "dp", None),
        P(),
    )
    out_specs = (
        P(("ep", "dp"), None),
        P(("ep", "dp"), None),
        P("ep", None, "dp"),
        P("ep", "dp", None),
    )
    return jax.shard_map(
        functools.partial(shards, geo),
        mesh=mesh,
        in_specs=in_specs,
        out_specs=out_specs,
        check_vma=False,
    )
```

```python
import functools

import jax
import jax.numpy as jnp
import numpy as np
from jax import lax
from jax.experimental import pallas as pl
from jax.experimental.pallas import tpu as pltpu
from jax.sharding import PartitionSpec as P

MESH = pl.DeviceIdType.MESH
NX = 4
CAP = 3
CHUNKS = 7
LEAD = 2
TILES = 3
SPANS = ((0, 2), (2, 5))
PIECES = 2
VMEM_LIMIT = 57 * 2**20
BF16 = jnp.bfloat16
F32 = jnp.float32
I32 = jnp.int32


def dot(left, right, dims=((1,), (0,))):
    return lax.dot_general(left, right, (dims, ((), ())), preferred_element_type=F32)


def loop(count, body):
    def run(i, _):
        body(i)
        return 0

    lax.fori_loop(0, count, run, 0)


class Geometry:
    def __init__(self, ny, nz):
        self.ny, self.nz = ny, nz
        self.zrows = ny * 2 * CAP
        self.yrows = 2 * nz * CAP
        self.xrows = ny * nz * CAP
        self.rows = 2 * self.xrows

    def matrices(self):
        ny, nz, rows = self.ny, self.nz, self.rows
        by_z = np.arange(rows).reshape(nz, ny, 2, CAP)
        by_y = np.arange(rows).reshape(ny, 2, nz, CAP)
        to_y = np.zeros((rows, rows), np.float32)
        to_y[np.arange(rows), by_z.transpose(1, 2, 0, 3).reshape(-1)] = 1
        to_x = np.zeros((rows, rows), np.float32)
        to_x[np.arange(rows), by_y.transpose(1, 0, 2, 3).reshape(-1)] = 1
        return [m.astype(jnp.bfloat16) for m in (to_y, to_y.T, to_x, to_x.T)]


def kernel(
    geo,
    tokens_in,
    cotangent_in,
    routes,
    probs,
    moving,
    up_in,
    down_in,
    to_y,
    from_y,
    to_x,
    from_x,
    tokens,
    cotangent,
    up,
    down,
    up_own,
    down_own,
    hidden_grad,
    hidden,
    slope,
    their_hidden,
    their_grad,
    select,
    unselect,
    sent,
    got_z,
    got_y,
    routed,
    part,
    core_part,
    x_part,
    back_y,
    back_z,
    send_sem,
    recv_sem,
    local_sem,
):
    ny, nz = geo.ny, geo.nz
    xr, yr, zr, rows = geo.xrows, geo.yrows, geo.zrows, geo.rows
    count, width = tokens.shape
    wide = width // CHUNKS
    ep, dp = lax.axis_index("ep"), lax.axis_index("dp")
    x_lo, y, z = ep // (ny * nz), (ep // nz) % ny, ep % nz
    x, core = (dp // 2) * 2 + x_lo, dp % 2

    def at(dx=0, dy=0, dz=0, dc=0):
        nx_, ny_, nz_ = (x + dx) % NX, (y + dy % ny) % ny, (z + dz % nz) % nz
        return ((nx_ % 2) * (ny * nz) + ny_ * nz + nz_, (nx_ // 2) * 2 + (core + dc) % 2)

    peers = (
        [at(dz=d) for d in range(1, nz)]
        + [at(dy=d) for d in range(1, ny)]
        + [at(dx=d) for d in range(1, NX)]
        + [at(dc=1)]
    )
    barrier = pltpu.get_barrier_semaphore()
    for peer in peers:
        pl.semaphore_signal(barrier, inc=1, device_id=peer, device_id_type=MESH)

    loads = [
        pltpu.make_async_copy(src, dst, local_sem.at[i])
        for i, (src, dst) in enumerate(
            (
                (tokens_in, tokens),
                (cotangent_in, cotangent),
                (up_in, up_own),
                (down_in, down_own),
            )
        )
    ]
    for load in loads:
        load.start()

    used = {}
    waiting = {}

    def start(key, src, dst, device):
        number = used.setdefault(key, len(used))
        copy = pltpu.make_async_remote_copy(
            src_ref=src,
            dst_ref=dst,
            send_sem=send_sem.at[number],
            recv_sem=recv_sem.at[number],
            device_id=device,
            device_id_type=MESH,
        )
        copy.start()
        waiting[id(copy)] = copy
        return copy

    def settle(copies):
        for copy in copies:
            copy.wait_send()
            del waiting[id(copy)]

    def y_block(d):
        return pl.ds(d * yr, yr)

    def x_block(d):
        return pl.ds(d * xr, xr)

    def chunk_cols(ch):
        return pl.ds(pl.multiple_of(ch * wide, wide), wide)

    half_count = ny * nz
    expert = routes[...]
    flip = jnp.zeros_like(expert)
    for pair in range(half_count):
        flip += jnp.where((expert & (half_count - 1)) == pair, moving[pair], 0)
    target_row = (expert + half_count * flip) & (2 * half_count - 1)
    down_iota = lax.broadcasted_iota(I32, (count, count), 0)
    across_iota = lax.broadcasted_iota(I32, (count, count), 1)

    def as_column(row):
        spread = jnp.where(down_iota == across_iota, row.astype(F32), 0.0)
        return jnp.sum(spread, axis=1, keepdims=True)

    target_column = as_column(target_row).astype(I32)
    same = target_column == target_row
    rank_row = jnp.sum(
        jnp.where(same & (down_iota < across_iota), 1.0, 0.0), axis=0, keepdims=True
    ).astype(I32)

    def slot_of(target, rank):
        dz = (target - z) & (nz - 1)
        dy = (target // nz - y) & (ny - 1)
        cross = (target // half_count) ^ x_lo
        return dz * zr + (dy * 2 + cross) * CAP + rank

    slot_row = slot_of(target_row, rank_row)
    slot_column = as_column(slot_row).astype(I32)
    select[...] = jnp.where(
        lax.broadcasted_iota(I32, (rows, count), 0) == slot_row, 1.0, 0.0
    ).astype(BF16)
    unselect[...] = jnp.where(
        lax.broadcasted_iota(I32, (count, rows), 1) == slot_column, 1.0, 0.0
    ).astype(BF16)
    weight = as_column(probs[...])

    def pick(s, first, number):
        def tile(i):
            ch = first + i
            cols = chunk_cols(ch)
            if s == 0:
                given = tokens[:, cols]
            else:
                given = (weight * cotangent[:, cols].astype(F32)).astype(BF16)
            block = dot(select[...], given).astype(BF16)
            for d in range(nz):
                sent[s, ch, d] = block[d * zr : (d + 1) * zr]
            got_z[s, ch, 0] = block[:zr]

        loop(number, tile)
        span = pl.ds(first, number)
        return [
            start(("z", s, first, d), sent.at[s, span, d], got_z.at[s, span, d], at(dz=d))
            for d in range(1, nz)
        ]

    def to_ring_y(s, first, number, copies):
        for copy in copies:
            copy.wait_recv()

        def tile(i):
            ch = first + i
            block = jnp.concatenate([got_z[s, ch, d] for d in range(nz)], axis=0)
            block = dot(to_y[...], block).astype(BF16)
            part[s, ch, pl.ds(0, rows), :] = block
            got_y[s, ch, y_block(0), :] = block[:yr]

        loop(number, tile)
        span = pl.ds(first, number)
        return [
            start(
                ("y", s, first, d),
                part.at[s, span, y_block(d)],
                got_y.at[s, span, y_block(d)],
                at(dy=d),
            )
            for d in range(1, ny)
        ]

    def to_ring_x(s, first, number, copies):
        for copy in copies:
            copy.wait_recv()

        def tile(i):
            ch = first + i
            block = dot(to_x[...], got_y[s, ch]).astype(BF16)
            routed[s, ch, x_block(0), :] = block[:xr]
            part[s, ch, pl.ds(rows, xr), :] = block[xr:]

        loop(number, tile)
        span = pl.ds(first, number)
        other = part.at[s, span, pl.ds(rows, xr)]
        own = routed.at[s, span, x_block(0)]
        return {
            1: start(("x", s, first, 1), other, routed.at[s, span, x_block(1)], at(dx=1)),
            3: start(("x", s, first, 3), other, routed.at[s, span, x_block(3)], at(dx=3)),
            2: start(("x", s, first, 2), own, routed.at[s, span, x_block(2)], at(dx=2)),
            0: start(("c", s, first, 0), own, routed.at[s, span, x_block(4)], at(dc=1)),
        }

    def share(s, first, number, made):
        shared = [made[0]]
        span = pl.ds(first, number)
        for d in (1, 3, 2):
            made[d].wait_recv()
            shared.append(
                start(
                    ("c", s, first, d),
                    routed.at[s, span, x_block(d)],
                    routed.at[s, span, x_block(4 + d)],
                    at(dc=1),
                )
            )
        return shared

    chosen = moving[ep % half_count] == 1

    def take_weights(swaps):
        for copy, load, buffer, own, parts in zip(
            swaps, loads[2:], (up, down), (up_own, down_own), (7, 4)
        ):
            load.wait()
            copy.wait_recv()
            step = buffer.shape[0] // parts

            def run(i, buffer=buffer, own=own, step=step):
                at_rows = pl.ds(pl.multiple_of(i * step, step), step)
                buffer[at_rows, :] = lax.select(chosen, buffer[at_rows, :], own[at_rows, :])

            loop(parts, run)

    def group(i):
        return pl.ds(pl.multiple_of(i * 4 * xr, 4 * xr), 4 * xr)

    def forward(shared):
        for copy in shared:
            copy.wait_recv()

        def run(i):
            value = dot(routed[0, 0, group(i), :], up[pl.ds(0, wide), :])
            for ch in range(1, CHUNKS):
                value += dot(routed[0, ch, group(i), :], up[pl.ds(ch * wide, wide), :])
            sigmoid = jax.nn.sigmoid(value)
            hidden[group(i), :] = (value * sigmoid).astype(BF16)
            slope[group(i), :] = sigmoid * (1.0 + value * (1.0 - sigmoid))

        loop(2, run)

    def backward(shared):
        for copy in shared:
            copy.wait_recv()
        over_cols = ((1,), (1,))

        def run(i):
            value = dot(routed[1, 0, group(i), :], down[:, pl.ds(0, wide)], over_cols)
            for ch in range(1, CHUNKS):
                cols = pl.ds(ch * wide, wide)
                value += dot(routed[1, ch, group(i), :], down[:, cols], over_cols)
            hidden_grad[group(i), :] = (value * slope[group(i), :]).astype(BF16)

        loop(2, run)

    def traded(s):
        mine, theirs = ((hidden, their_hidden), (hidden_grad, their_grad))[s]
        copies = []
        for block, other in ((0, 2), (2, 0), (4, 6), (6, 4)):
            number = used.setdefault(("t", s, block), len(used))
            copies.append(
                pltpu.make_async_remote_copy(
                    src_ref=mine.at[pl.ds(block * xr, 2 * xr)],
                    dst_ref=theirs.at[pl.ds(other * xr, 2 * xr)],
                    send_sem=send_sem.at[number],
                    recv_sem=recv_sem.at[number],
                    device_id=at(dx=2),
                    device_id_type=MESH,
                )
            )
        return copies

    def trade(s):
        @pl.when(core == 1)
        def _():
            for copy in traded(s):
                copy.start()

    def take_traded(s):
        mine, theirs = ((hidden, their_hidden), (hidden_grad, their_grad))[s]

        @pl.when(core == 1)
        def _():
            for copy in traded(s):
                copy.wait()

            def run(i):
                mine[group(i), :] = lax.select(chosen, theirs[group(i), :], mine[group(i), :])

            loop(2, run)

    def parts(s, ch):
        def run(i):
            if s == 0:
                block = dot(hidden[group(i), :], down[:, pl.ds(ch * wide, wide)])
            else:
                block = dot(
                    hidden_grad[group(i), :], up[pl.ds(ch * wide, wide), :], ((1,), (1,))
                )
            part[s, ch, group(i), :] = block.astype(BF16)

        loop(2, run)
        far = part.at[s, ch, pl.ds(4 * xr, 4 * xr)]
        return start(("p", s, ch), far, core_part.at[s, ch], at(dc=1))

    def chip_sum(s, ch, copy):
        copy.wait_recv()

        def run(i):
            block = x_block_at(i)
            total = part[s, ch, block, :].astype(F32) + core_part[s, ch, block, :].astype(F32)
            part[s, ch, block, :] = total.astype(BF16)

        loop(4, run)
        return [
            start(
                ("b", s, ch, d),
                part.at[s, ch, x_block(d)],
                x_part.at[s, ch, x_block(place)],
                at(dx=NX - d),
            )
            for d, place in ((1, 1), (3, 2), (2, 0))
        ]

    def x_block_at(i):
        return pl.ds(pl.multiple_of(i * xr, xr), xr)

    def from_ring_x(s, ch, copies):
        for copy in copies:
            copy.wait_recv()
        taken = [x_part[s, ch, x_block(i), :].astype(F32) for i in range(3)]
        same_x = (part[s, ch, x_block(0), :].astype(F32) + taken[0]).astype(BF16)
        cross_x = (taken[1] + taken[2]).astype(BF16)
        block = dot(from_x[...], jnp.concatenate([same_x, cross_x], axis=0)).astype(BF16)
        got_y[s, ch] = block
        back_y[s, ch, y_block(0), :] = block[:yr]
        return [
            start(
                ("v", s, ch, d),
                got_y.at[s, ch, y_block(d)],
                back_y.at[s, ch, y_block(d)],
                at(dy=-d),
            )
            for d in range(1, ny)
        ]

    def from_ring_y(s, ch, copies):
        for copy in copies:
            copy.wait_recv()
        block = dot(from_y[...], back_y[s, ch]).astype(BF16)
        for d in range(nz):
            sent[s, ch, d] = block[d * zr : (d + 1) * zr]
        back_z[s, ch, 0] = block[:zr]
        return [
            start(("w", s, ch, d), sent.at[s, ch, d], back_z.at[s, ch, d], at(dz=-d))
            for d in range(1, nz)
        ]

    def finish(s, ch, copies):
        for copy in copies:
            copy.wait_recv()
        block = jnp.concatenate([back_z[s, ch, d] for d in range(nz)], axis=0)
        picked = dot(unselect[...], block)
        out = (tokens, cotangent)[s]
        out[:, pl.ds(ch * wide, wide)] = (picked if s else weight * picked).astype(BF16)

    def up_tile(ch):
        cols = chunk_cols(ch)
        up[cols, :] = dot(routed[0, ch], hidden_grad[...], ((0,), (0,))).astype(BF16)

    def down_tile(ch):
        cols = pl.ds(ch * wide, wide)
        down[:, cols] = dot(hidden[...], routed[1, ch], ((0,), (0,))).astype(BF16)

    pl.semaphore_wait(barrier, len(peers))
    swaps = [
        start(("s", i), own, buffer, at(dx=1 + 2 * (x_lo ^ core)))
        for i, (own, buffer) in enumerate(((up_in, up), (down_in, down)))
    ]
    streams = [(s, *span) for s in range(2) for span in SPANS]
    along_z, along_y, along_x, shared = [], [], [], ([], [])
    for s, first, number in streams:
        if first == 0:
            loads[s].wait()
        along_z.append(pick(s, first, number))
    for stream, copies in zip(streams, along_z):
        along_y.append(to_ring_y(*stream, copies))
        along_x.append(to_ring_x(*stream, along_y[-1]))
        done = len(along_x) - 3
        if done >= 0:
            shared[0].extend(share(*streams[done], along_x[done]))
    from_part = [along_y[i] + [along_x[i][1], along_x[i][3]] for i in range(4)]
    take_weights(swaps)
    settle(from_part[0] + from_part[1])
    forward(shared[0])
    trade(0)
    part_sent = [parts(0, ch) for ch in range(CHUNKS)]
    items = [(s, ch) for s in range(2) for ch in range(CHUNKS)]
    x_given, y_given, z_given = {}, {}, {}
    for i in range(LEAD):
        x_given[i] = chip_sum(*items[i], part_sent[i])
    for done in (2, 3):
        shared[1].extend(share(*streams[done], along_x[done]))
    settle(from_part[2] + from_part[3])
    backward(shared[1])
    for copies in along_z:
        settle(copies)
    tiles = [functools.partial(take_traded, 0)]
    tiles += [functools.partial(down_tile, ch) for ch in range(CHUNKS)]
    for i in range(LEAD, len(items) + LEAD + 4):
        x_done, y_done, z_done = i - LEAD, i - LEAD - 1, i - LEAD - 4
        if x_done in x_given:
            y_given[x_done] = from_ring_x(*items[x_done], x_given[x_done])
            if x_done == len(items) - 1:
                trade(1)
        if i < len(items):
            x_given[i] = chip_sum(*items[i], part_sent[i])
        if i - LEAD < CHUNKS:
            part_sent.append(parts(1, i - LEAD))
        if y_done in y_given:
            z_given[y_done] = from_ring_y(*items[y_done], y_given[y_done])
            if y_done == len(items) - 1:
                take_traded(1)
                loop(CHUNKS, up_tile)
        if i - LEAD >= CHUNKS - 1:
            for _ in range(min(TILES, len(tiles))):
                tiles.pop(0)()
        if z_done in z_given:
            finish(*items[z_done], z_given[z_done])
    settle(list(waiting.values()))


def place(*refs):
    copies = []
    for i, (source, target) in enumerate(zip(refs[:4], refs[4:8])):
        step = source.shape[0] // PIECES
        for j in range(PIECES):
            rows = pl.ds(j * step, step)
            copies.append(
                pltpu.make_async_copy(
                    source.at[rows], target.at[rows], refs[8].at[PIECES * i + j]
                )
            )
            copies[-1].start()
    for copy in copies:
        copy.wait()


def shards(geo, tokens, cotangent, routes, router_probs, up_weight, down_weight, moving):
    ny, nz = geo.ny, geo.nz
    count, width = tokens.shape
    hid = up_weight.shape[2]
    rows, xr, wide = geo.rows, geo.xrows, width // CHUNKS
    vmem = pl.BlockSpec(memory_space=pltpu.VMEM)
    smem = pl.BlockSpec(memory_space=pltpu.SMEM)
    anywhere = pl.BlockSpec(memory_space=pl.ANY)
    out_copies = len(SPANS) * (nz - 1 + ny - 1 + 3 + 4)
    copies = 2 * (out_copies + CHUNKS * (1 + 3 + ny - 1 + nz - 1) + 4) + 2
    buffer = lambda *shape: pltpu.VMEM(shape, BF16)
    results = pl.pallas_call(
        functools.partial(kernel, geo),
        out_shape=(
            buffer(count, width),
            buffer(count, width),
            buffer(width, hid),
            buffer(hid, width),
        ),
        in_specs=[anywhere, anywhere, vmem, vmem, smem, anywhere, anywhere] + [vmem] * 4,
        out_specs=(vmem,) * 4,
        scratch_shapes=[
            buffer(width, hid),
            buffer(hid, width),
            buffer(8 * xr, hid),
            buffer(8 * xr, hid),
            pltpu.VMEM((8 * xr, hid), F32),
            buffer(8 * xr, hid),
            buffer(8 * xr, hid),
            buffer(rows, count),
            buffer(count, rows),
            buffer(2, CHUNKS, nz, geo.zrows, wide),
            buffer(2, CHUNKS, nz, geo.zrows, wide),
            buffer(2, CHUNKS, rows, wide),
            buffer(2, CHUNKS, 8 * xr, wide),
            buffer(2, CHUNKS, 8 * xr, wide),
            buffer(2, CHUNKS, 4 * xr, wide),
            buffer(2, CHUNKS, 3 * xr, wide),
            buffer(2, CHUNKS, rows, wide),
            buffer(2, CHUNKS, nz, geo.zrows, wide),
            pltpu.SemaphoreType.DMA((copies,)),
            pltpu.SemaphoreType.DMA((copies,)),
            pltpu.SemaphoreType.DMA((4,)),
        ],
        compiler_params=pltpu.CompilerParams(
            collective_id=0, has_side_effects=True, vmem_limit_bytes=VMEM_LIMIT
        ),
    )(
        tokens,
        cotangent,
        routes.reshape(1, count),
        router_probs.reshape(1, count),
        moving,
        up_weight[0],
        down_weight[0],
        *[jnp.asarray(m) for m in geo.matrices()],
    )
    outputs, input_grad, up_grad, down_grad = pl.pallas_call(
        place,
        out_shape=[jax.ShapeDtypeStruct(r.shape, r.dtype) for r in results],
        in_specs=[anywhere] * 4,
        out_specs=[anywhere] * 4,
        scratch_shapes=[pltpu.SemaphoreType.DMA((4 * PIECES,))],
        compiler_params=pltpu.CompilerParams(vmem_limit_bytes=2**20),
    )(*results)
    return outputs, input_grad, up_grad[None], down_grad[None]


def solution(mesh):
    ep_count = mesh.shape["ep"]
    nz = 8 if ep_count == 64 else 2
    geo = Geometry(ep_count // 2 // nz, nz)
    in_specs = (
        P(("ep", "dp"), None),
        P(("ep", "dp"), None),
        P(("ep", "dp"), None),
        P(("ep", "dp"), None),
        P("ep", None, "dp"),
        P("ep", "dp", None),
        P(),
    )
    out_specs = (
        P(("ep", "dp"), None),
        P(("ep", "dp"), None),
        P("ep", None, "dp"),
        P("ep", "dp", None),
    )
    return jax.shard_map(
        functools.partial(shards, geo),
        mesh=mesh,
        in_specs=in_specs,
        out_specs=out_specs,
        check_vma=False,
    )
```

```python
import functools

import jax
import jax.numpy as jnp
import numpy as np
from jax import lax
from jax.experimental import pallas as pl
from jax.experimental.pallas import tpu as pltpu
from jax.sharding import PartitionSpec as P

MESH = pl.DeviceIdType.MESH
NX = 4
CAP = 3
CHUNKS = 7
LEAD = 3
SPANS = ((0, 2), (2, 5))
PIECES = 2
VMEM_LIMIT = 57 * 2**20
BF16 = jnp.bfloat16
F32 = jnp.float32
I32 = jnp.int32


def dot(left, right, dims=((1,), (0,))):
    return lax.dot_general(left, right, (dims, ((), ())), preferred_element_type=F32)


def loop(count, body):
    def run(i, _):
        body(i)
        return 0

    lax.fori_loop(0, count, run, 0)


class Geometry:
    def __init__(self, ny, nz):
        self.ny, self.nz = ny, nz
        self.zrows = ny * 2 * CAP
        self.yrows = 2 * nz * CAP
        self.xrows = ny * nz * CAP
        self.rows = 2 * self.xrows

    def matrices(self):
        ny, nz, rows = self.ny, self.nz, self.rows
        by_z = np.arange(rows).reshape(nz, ny, 2, CAP)
        by_y = np.arange(rows).reshape(ny, 2, nz, CAP)
        to_y = np.zeros((rows, rows), np.float32)
        to_y[np.arange(rows), by_z.transpose(1, 2, 0, 3).reshape(-1)] = 1
        to_x = np.zeros((rows, rows), np.float32)
        to_x[np.arange(rows), by_y.transpose(1, 0, 2, 3).reshape(-1)] = 1
        return [m.astype(jnp.bfloat16) for m in (to_y, to_y.T, to_x, to_x.T)]


def kernel(
    geo,
    tokens_in,
    cotangent_in,
    routes,
    probs,
    moving,
    up_in,
    down_in,
    to_y,
    from_y,
    to_x,
    from_x,
    tokens,
    cotangent,
    up,
    down,
    up_own,
    down_own,
    hidden_grad,
    hidden,
    slope,
    their_hidden,
    their_grad,
    select,
    unselect,
    sent,
    got_z,
    got_y,
    routed,
    part,
    core_part,
    x_part,
    back_y,
    back_z,
    send_sem,
    recv_sem,
    local_sem,
):
    ny, nz = geo.ny, geo.nz
    xr, yr, zr, rows = geo.xrows, geo.yrows, geo.zrows, geo.rows
    count, width = tokens.shape
    wide = width // CHUNKS
    ep, dp = lax.axis_index("ep"), lax.axis_index("dp")
    x_lo, y, z = ep // (ny * nz), (ep // nz) % ny, ep % nz
    x, core = (dp // 2) * 2 + x_lo, dp % 2

    def at(dx=0, dy=0, dz=0, dc=0):
        nx_, ny_, nz_ = (x + dx) % NX, (y + dy % ny) % ny, (z + dz % nz) % nz
        return ((nx_ % 2) * (ny * nz) + ny_ * nz + nz_, (nx_ // 2) * 2 + (core + dc) % 2)

    peers = (
        [at(dz=d) for d in range(1, nz)]
        + [at(dy=d) for d in range(1, ny)]
        + [at(dx=d) for d in range(1, NX)]
        + [at(dc=1)]
    )
    barrier = pltpu.get_barrier_semaphore()
    for peer in peers:
        pl.semaphore_signal(barrier, inc=1, device_id=peer, device_id_type=MESH)

    loads = [
        pltpu.make_async_copy(src, dst, local_sem.at[i])
        for i, (src, dst) in enumerate(
            (
                (tokens_in, tokens),
                (cotangent_in, cotangent),
                (up_in, up_own),
                (down_in, down_own),
            )
        )
    ]
    for load in loads:
        load.start()

    used = {}
    waiting = {}

    def start(key, src, dst, device):
        number = used.setdefault(key, len(used))
        copy = pltpu.make_async_remote_copy(
            src_ref=src,
            dst_ref=dst,
            send_sem=send_sem.at[number],
            recv_sem=recv_sem.at[number],
            device_id=device,
            device_id_type=MESH,
        )
        copy.start()
        waiting[id(copy)] = copy
        return copy

    def settle(copies):
        for copy in copies:
            copy.wait_send()
            del waiting[id(copy)]

    def y_block(d):
        return pl.ds(d * yr, yr)

    def x_block(d):
        return pl.ds(d * xr, xr)

    def chunk_cols(ch):
        return pl.ds(pl.multiple_of(ch * wide, wide), wide)

    half_count = ny * nz
    expert = routes[...]
    flip = jnp.zeros_like(expert)
    for pair in range(half_count):
        flip += jnp.where((expert & (half_count - 1)) == pair, moving[pair], 0)
    target_row = (expert + half_count * flip) & (2 * half_count - 1)
    down_iota = lax.broadcasted_iota(I32, (count, count), 0)
    across_iota = lax.broadcasted_iota(I32, (count, count), 1)

    def as_column(row):
        spread = jnp.where(down_iota == across_iota, row.astype(F32), 0.0)
        return jnp.sum(spread, axis=1, keepdims=True)

    target_column = as_column(target_row).astype(I32)
    same = target_column == target_row
    rank_row = jnp.sum(
        jnp.where(same & (down_iota < across_iota), 1.0, 0.0), axis=0, keepdims=True
    ).astype(I32)

    def slot_of(target, rank):
        dz = (target - z) & (nz - 1)
        dy = (target // nz - y) & (ny - 1)
        cross = (target // half_count) ^ x_lo
        return dz * zr + (dy * 2 + cross) * CAP + rank

    slot_row = slot_of(target_row, rank_row)
    slot_column = as_column(slot_row).astype(I32)
    select[...] = jnp.where(
        lax.broadcasted_iota(I32, (rows, count), 0) == slot_row, 1.0, 0.0
    ).astype(BF16)
    unselect[...] = jnp.where(
        lax.broadcasted_iota(I32, (count, rows), 1) == slot_column, 1.0, 0.0
    ).astype(BF16)
    weight = as_column(probs[...])

    def pick(s, first, number):
        def tile(i):
            ch = first + i
            cols = chunk_cols(ch)
            if s == 0:
                given = tokens[:, cols]
            else:
                given = (weight * cotangent[:, cols].astype(F32)).astype(BF16)
            block = dot(select[...], given).astype(BF16)
            for d in range(nz):
                sent[s, ch, d] = block[d * zr : (d + 1) * zr]
            got_z[s, ch, 0] = block[:zr]

        loop(number, tile)
        span = pl.ds(first, number)
        return [
            start(("z", s, first, d), sent.at[s, span, d], got_z.at[s, span, d], at(dz=d))
            for d in range(1, nz)
        ]

    def to_ring_y(s, first, number, copies):
        for copy in copies:
            copy.wait_recv()

        def tile(i):
            ch = first + i
            block = jnp.concatenate([got_z[s, ch, d] for d in range(nz)], axis=0)
            block = dot(to_y[...], block).astype(BF16)
            part[s, ch, pl.ds(0, rows), :] = block
            got_y[s, ch, y_block(0), :] = block[:yr]

        loop(number, tile)
        span = pl.ds(first, number)
        return [
            start(
                ("y", s, first, d),
                part.at[s, span, y_block(d)],
                got_y.at[s, span, y_block(d)],
                at(dy=d),
            )
            for d in range(1, ny)
        ]

    def to_ring_x(s, first, number, copies):
        for copy in copies:
            copy.wait_recv()

        def tile(i):
            ch = first + i
            block = dot(to_x[...], got_y[s, ch]).astype(BF16)
            routed[s, ch, x_block(0), :] = block[:xr]
            part[s, ch, pl.ds(rows, xr), :] = block[xr:]

        loop(number, tile)
        span = pl.ds(first, number)
        other = part.at[s, span, pl.ds(rows, xr)]
        own = routed.at[s, span, x_block(0)]
        return {
            1: start(("x", s, first, 1), other, routed.at[s, span, x_block(1)], at(dx=1)),
            3: start(("x", s, first, 3), other, routed.at[s, span, x_block(3)], at(dx=3)),
            2: start(("x", s, first, 2), own, routed.at[s, span, x_block(2)], at(dx=2)),
            0: start(("c", s, first, 0), own, routed.at[s, span, x_block(4)], at(dc=1)),
        }

    def share(s, first, number, made):
        shared = [made[0]]
        span = pl.ds(first, number)
        for d in (1, 3, 2):
            made[d].wait_recv()
            shared.append(
                start(
                    ("c", s, first, d),
                    routed.at[s, span, x_block(d)],
                    routed.at[s, span, x_block(4 + d)],
                    at(dc=1),
                )
            )
        return shared

    chosen = moving[ep % half_count] == 1

    def take_weights(swaps):
        for copy, load, buffer, own, parts in zip(
            swaps, loads[2:], (up, down), (up_own, down_own), (7, 4)
        ):
            load.wait()
            copy.wait_recv()
            step = buffer.shape[0] // parts

            def run(i, buffer=buffer, own=own, step=step):
                at_rows = pl.ds(pl.multiple_of(i * step, step), step)
                buffer[at_rows, :] = lax.select(chosen, buffer[at_rows, :], own[at_rows, :])

            loop(parts, run)

    def group(i):
        return pl.ds(pl.multiple_of(i * 4 * xr, 4 * xr), 4 * xr)

    def forward(shared):
        for copy in shared:
            copy.wait_recv()

        def run(i):
            value = dot(routed[0, 0, group(i), :], up[pl.ds(0, wide), :])
            for ch in range(1, CHUNKS):
                value += dot(routed[0, ch, group(i), :], up[pl.ds(ch * wide, wide), :])
            sigmoid = jax.nn.sigmoid(value)
            hidden[group(i), :] = (value * sigmoid).astype(BF16)
            slope[group(i), :] = sigmoid * (1.0 + value * (1.0 - sigmoid))

        loop(2, run)

    def backward(shared):
        for copy in shared:
            copy.wait_recv()
        over_cols = ((1,), (1,))

        def run(i):
            value = dot(routed[1, 0, group(i), :], down[:, pl.ds(0, wide)], over_cols)
            for ch in range(1, CHUNKS):
                cols = pl.ds(ch * wide, wide)
                value += dot(routed[1, ch, group(i), :], down[:, cols], over_cols)
            hidden_grad[group(i), :] = (value * slope[group(i), :]).astype(BF16)

        loop(2, run)

    def traded(s):
        mine, theirs = ((hidden, their_hidden), (hidden_grad, their_grad))[s]
        copies = []
        for block, other in ((0, 2), (2, 0), (4, 6), (6, 4)):
            number = used.setdefault(("t", s, block), len(used))
            copies.append(
                pltpu.make_async_remote_copy(
                    src_ref=mine.at[pl.ds(block * xr, 2 * xr)],
                    dst_ref=theirs.at[pl.ds(other * xr, 2 * xr)],
                    send_sem=send_sem.at[number],
                    recv_sem=recv_sem.at[number],
                    device_id=at(dx=2),
                    device_id_type=MESH,
                )
            )
        return copies

    def trade(s):
        @pl.when(core == 1)
        def _():
            for copy in traded(s):
                copy.start()

    def take_traded(s):
        mine, theirs = ((hidden, their_hidden), (hidden_grad, their_grad))[s]

        @pl.when(core == 1)
        def _():
            for copy in traded(s):
                copy.wait()

            def run(i):
                mine[group(i), :] = lax.select(chosen, theirs[group(i), :], mine[group(i), :])

            loop(2, run)

    def parts(s, ch):
        def run(i):
            if s == 0:
                block = dot(hidden[group(i), :], down[:, pl.ds(ch * wide, wide)])
            else:
                block = dot(
                    hidden_grad[group(i), :], up[pl.ds(ch * wide, wide), :], ((1,), (1,))
                )
            part[s, ch, group(i), :] = block.astype(BF16)

        loop(2, run)
        far = part.at[s, ch, pl.ds(4 * xr, 4 * xr)]
        return start(("p", s, ch), far, core_part.at[s, ch], at(dc=1))

    def chip_sum(s, ch, copy):
        copy.wait_recv()

        def run(i):
            block = x_block_at(i)
            total = part[s, ch, block, :].astype(F32) + core_part[s, ch, block, :].astype(F32)
            part[s, ch, block, :] = total.astype(BF16)

        loop(4, run)
        return [
            start(
                ("b", s, ch, d),
                part.at[s, ch, x_block(d)],
                x_part.at[s, ch, x_block(place)],
                at(dx=NX - d),
            )
            for d, place in ((1, 1), (3, 2), (2, 0))
        ]

    def x_block_at(i):
        return pl.ds(pl.multiple_of(i * xr, xr), xr)

    def from_ring_x(s, ch, copies):
        for copy in copies:
            copy.wait_recv()
        taken = [x_part[s, ch, x_block(i), :].astype(F32) for i in range(3)]
        same_x = (part[s, ch, x_block(0), :].astype(F32) + taken[0]).astype(BF16)
        cross_x = (taken[1] + taken[2]).astype(BF16)
        block = dot(from_x[...], jnp.concatenate([same_x, cross_x], axis=0)).astype(BF16)
        got_y[s, ch] = block
        back_y[s, ch, y_block(0), :] = block[:yr]
        return [
            start(
                ("v", s, ch, d),
                got_y.at[s, ch, y_block(d)],
                back_y.at[s, ch, y_block(d)],
                at(dy=-d),
            )
            for d in range(1, ny)
        ]

    def from_ring_y(s, ch, copies):
        for copy in copies:
            copy.wait_recv()
        block = dot(from_y[...], back_y[s, ch]).astype(BF16)
        for d in range(nz):
            sent[s, ch, d] = block[d * zr : (d + 1) * zr]
        back_z[s, ch, 0] = block[:zr]
        return [
            start(("w", s, ch, d), sent.at[s, ch, d], back_z.at[s, ch, d], at(dz=-d))
            for d in range(1, nz)
        ]

    def finish(s, ch, copies):
        for copy in copies:
            copy.wait_recv()
        block = jnp.concatenate([back_z[s, ch, d] for d in range(nz)], axis=0)
        picked = dot(unselect[...], block)
        out = (tokens, cotangent)[s]
        out[:, pl.ds(ch * wide, wide)] = (picked if s else weight * picked).astype(BF16)

    def up_tile(ch):
        cols = chunk_cols(ch)
        up[cols, :] = dot(routed[0, ch], hidden_grad[...], ((0,), (0,))).astype(BF16)

    def down_tile(ch):
        cols = chunk_cols(ch)
        down[:, cols] = dot(hidden[...], routed[1, ch], ((0,), (0,))).astype(BF16)

    pl.semaphore_wait(barrier, len(peers))
    swaps = [
        start(("s", i), own, buffer, at(dx=1 + 2 * (x_lo ^ core)))
        for i, (own, buffer) in enumerate(((up_in, up), (down_in, down)))
    ]
    streams = [(s, *span) for s in range(2) for span in SPANS]
    along_z, along_y, along_x, shared = [], [], [], ([], [])
    for s, first, number in streams:
        if first == 0:
            loads[s].wait()
        along_z.append(pick(s, first, number))
    for stream, copies in zip(streams, along_z):
        along_y.append(to_ring_y(*stream, copies))
        along_x.append(to_ring_x(*stream, along_y[-1]))
        done = len(along_x) - 3
        if done >= 0:
            shared[0].extend(share(*streams[done], along_x[done]))
    from_part = [along_y[i] + [along_x[i][1], along_x[i][3]] for i in range(4)]
    take_weights(swaps)
    settle(from_part[0] + from_part[1])
    forward(shared[0])
    part_sent = [parts(0, ch) for ch in range(CHUNKS)]
    items = [(s, ch) for s in range(2) for ch in range(CHUNKS)]
    x_given, y_given, z_given = {}, {}, {}
    for i in range(LEAD):
        x_given[i] = chip_sum(*items[i], part_sent[i])
    for done in (2, 3):
        shared[1].extend(share(*streams[done], along_x[done]))
    settle(from_part[2] + from_part[3])
    backward(shared[1])
    for copies in along_z:
        settle(copies)
    for i in range(LEAD, len(items) + LEAD + 4):
        x_done, y_done, z_done = i - LEAD, i - LEAD - 1, i - LEAD - 4
        if x_done in x_given:
            y_given[x_done] = from_ring_x(*items[x_done], x_given[x_done])
            if x_done == len(items) - 1:
                trade(0)
                trade(1)
        if i < len(items):
            x_given[i] = chip_sum(*items[i], part_sent[i])
        if i - LEAD < CHUNKS:
            part_sent.append(parts(1, i - LEAD))
        if y_done in y_given:
            z_given[y_done] = from_ring_y(*items[y_done], y_given[y_done])
            if y_done == len(items) - 1:
                take_traded(0)
                loop(CHUNKS, down_tile)
                take_traded(1)
                loop(CHUNKS, up_tile)
        if z_done in z_given:
            finish(*items[z_done], z_given[z_done])
    settle(list(waiting.values()))


def place(*refs):
    copies = []
    for i, (source, target) in enumerate(zip(refs[:4], refs[4:8])):
        step = source.shape[0] // PIECES
        for j in range(PIECES):
            rows = pl.ds(j * step, step)
            copies.append(
                pltpu.make_async_copy(
                    source.at[rows], target.at[rows], refs[8].at[PIECES * i + j]
                )
            )
            copies[-1].start()
    for copy in copies:
        copy.wait()


def shards(geo, tokens, cotangent, routes, router_probs, up_weight, down_weight, moving):
    ny, nz = geo.ny, geo.nz
    count, width = tokens.shape
    hid = up_weight.shape[2]
    rows, xr, wide = geo.rows, geo.xrows, width // CHUNKS
    vmem = pl.BlockSpec(memory_space=pltpu.VMEM)
    smem = pl.BlockSpec(memory_space=pltpu.SMEM)
    anywhere = pl.BlockSpec(memory_space=pl.ANY)
    out_copies = len(SPANS) * (nz - 1 + ny - 1 + 3 + 4)
    copies = 2 * (out_copies + CHUNKS * (1 + 3 + ny - 1 + nz - 1) + 4) + 2
    buffer = lambda *shape: pltpu.VMEM(shape, BF16)
    results = pl.pallas_call(
        functools.partial(kernel, geo),
        out_shape=(
            buffer(count, width),
            buffer(count, width),
            buffer(width, hid),
            buffer(hid, width),
        ),
        in_specs=[anywhere, anywhere, vmem, vmem, smem, anywhere, anywhere] + [vmem] * 4,
        out_specs=(vmem,) * 4,
        scratch_shapes=[
            buffer(width, hid),
            buffer(hid, width),
            buffer(8 * xr, hid),
            buffer(8 * xr, hid),
            pltpu.VMEM((8 * xr, hid), F32),
            buffer(8 * xr, hid),
            buffer(8 * xr, hid),
            buffer(rows, count),
            buffer(count, rows),
            buffer(2, CHUNKS, nz, geo.zrows, wide),
            buffer(2, CHUNKS, nz, geo.zrows, wide),
            buffer(2, CHUNKS, rows, wide),
            buffer(2, CHUNKS, 8 * xr, wide),
            buffer(2, CHUNKS, 8 * xr, wide),
            buffer(2, CHUNKS, 4 * xr, wide),
            buffer(2, CHUNKS, 3 * xr, wide),
            buffer(2, CHUNKS, rows, wide),
            buffer(2, CHUNKS, nz, geo.zrows, wide),
            pltpu.SemaphoreType.DMA((copies,)),
            pltpu.SemaphoreType.DMA((copies,)),
            pltpu.SemaphoreType.DMA((4,)),
        ],
        compiler_params=pltpu.CompilerParams(
            collective_id=0, has_side_effects=True, vmem_limit_bytes=VMEM_LIMIT
        ),
    )(
        tokens,
        cotangent,
        routes.reshape(1, count),
        router_probs.reshape(1, count),
        moving,
        up_weight[0],
        down_weight[0],
        *[jnp.asarray(m) for m in geo.matrices()],
    )
    outputs, input_grad, up_grad, down_grad = pl.pallas_call(
        place,
        out_shape=[jax.ShapeDtypeStruct(r.shape, r.dtype) for r in results],
        in_specs=[anywhere] * 4,
        out_specs=[anywhere] * 4,
        scratch_shapes=[pltpu.SemaphoreType.DMA((4 * PIECES,))],
        compiler_params=pltpu.CompilerParams(vmem_limit_bytes=2**20),
    )(*results)
    return outputs, input_grad, up_grad[None], down_grad[None]


def solution(mesh):
    ep_count = mesh.shape["ep"]
    nz = 8 if ep_count == 64 else 2
    geo = Geometry(ep_count // 2 // nz, nz)
    in_specs = (
        P(("ep", "dp"), None),
        P(("ep", "dp"), None),
        P(("ep", "dp"), None),
        P(("ep", "dp"), None),
        P("ep", None, "dp"),
        P("ep", "dp", None),
        P(),
    )
    out_specs = (
        P(("ep", "dp"), None),
        P(("ep", "dp"), None),
        P("ep", None, "dp"),
        P("ep", "dp", None),
    )
    return jax.shard_map(
        functools.partial(shards, geo),
        mesh=mesh,
        in_specs=in_specs,
        out_specs=out_specs,
        check_vma=False,
    )
```
